32 devices in a mesh: dp: 8 (over z, x), head: 4 (over y, core).
Axes of the slice: x: 2, y: 2, z: 4, core: 2. Of those that a mesh axis runs over, the one named last changes fastest.
Arguments:
- tokens: bfloat16 [4096, 768], P(('dp', 'head')), may hold values from -6 to 6
- segments: int32 [8, 512], P('dp'), may hold values from 0 to 3, never falling along the last dimension, each value on 1 to 256 neighbouring positions
- routes: int32 [4096, 1], P(('dp', 'head')), may hold values from 0 to 1; in each aligned block of 128 rows (0 to 127, 128 to 255, ...) at most 96 rows name the same one
- norm_gain: bfloat16 [2, 2, 2, 768], P(None, None, None, 'dp'), may hold values from 0.25 to 1.75
- norm_bias: bfloat16 [2, 2, 2, 768], P(None, None, None, 'dp'), may hold values from -3 to 3
- w_qkv: bfloat16 [2, 768, 2304], P(None, 'dp'), may hold values from -0.21875 to 0.21875
- w_out: bfloat16 [2, 768, 768], P(None, 'dp'), may hold values from -0.625 to 0.625
- w_up: bfloat16 [2, 2, 768, 3072], P(None, None, 'dp'), may hold values from -0.21875 to 0.21875
- w_down: bfloat16 [2, 2, 3072, 768], P(None, None, 'dp'), may hold values from -0.15625 to 0.15625
- cotangent: bfloat16 [4096, 768], P(('dp', 'head')), may hold values from -6 to 6
Outputs:
- output: float32 [4096, 768], P(('dp', 'head'))
- grad_input: float32 [4096, 768], P(('dp', 'head'))
- grad_norm_gain: float32 [2, 2, 2, 768], P(None, None, None, 'dp')
- grad_norm_bias: float32 [2, 2, 2, 768], P(None, None, None, 'dp')
- grad_qkv: float32 [2, 768, 2304], P(None, 'dp')
- grad_out: float32 [2, 768, 768], P(None, 'dp')
- grad_up: float32 [2, 2, 768, 3072], P(None, None, 'dp')
- grad_down: float32 [2, 2, 3072, 768], P(None, None, 'dp')
The draws below stay inside these ranges and needn't reach their ends.
Inputs may be any that keep to these rules, and one draw needn't show every extreme that they name: `segments`: along each row the ids never fall, every id appears, and each document covers at most half of 512 positions; one covers exactly that many. `routes`: in the rows of one device no expert is named by more than 96 rows.
All inputs are finite; a program needn't handle non-finite values.
Results may differ from the reference program's by a relative error of at most 0.015.
Values may be sent and summed in bfloat16 or wider, within the bound.
No kernel may reach another device: no remote copies, remote signals or barrier semaphores. Data moves between devices by JAX's collectives and lax.ppermute only.
A program may use at most 256 MiB of HBM per device.

```python
import math
import jax
import jax.numpy as jnp
import numpy as np
from jax import lax

D = 768
H = 12
HD = 64
FF = 3072
LAYERS = 2
EXPERTS = 2
LEN = 512
SEGS = 4
TOK_DEV = 128
MOST = 96
ROWS = 8
TOKENS = 4096


def raised(drawn, stream_key, source, target, blocks, factor):
    def block_of(axis_at):
        return (jnp.arange(drawn.shape[axis_at]) // (drawn.shape[axis_at] // blocks)).reshape((-1,) + (1,) * (drawn.ndim - 1 - axis_at))

    near = jax.random.permutation(stream_key, blocks)[block_of(target)]
    other_side = (block_of(target) + blocks // 2) % blocks
    return jnp.where((block_of(source) == near) | (block_of(source) == other_side), factor * drawn, drawn)


def block_levels(rng, dims, pieces, least, largest):
    def one(dim, blocks):
        heights = jax.random.uniform(jax.random.fold_in(jax.random.fold_in(rng, 6), dim), (blocks,), jnp.float32, least / len(pieces), largest / len(pieces))
        return jnp.repeat(jnp.exp(heights), dims[dim] // blocks).reshape((-1,) + (1,) * (len(dims) - dim - 1))

    loudness = one(*pieces[0])
    for cut in pieces[1:]:
        loudness = loudness * one(*cut)
    return loudness


def profile(count, total, reach, slope):
    weights = [(1 << 20) // math.isqrt(standing ** slope) + 1 for standing in range(2, count + 1)]
    spare, holding = total - reach - (count - 1), [1] * (count - 1)
    while spare > 0:
        movable = [i for i in range(count - 1) if holding[i] < reach]
        mass, left = sum([weights[i] for i in movable]), spare
        for i in movable:
            more = min(reach - holding[i], max(1, left * weights[i] // mass), spare)
            holding[i] = holding[i] + more
            spare = spare - more
    return np.array([reach] + holding)


def ragged_sizes(rng, count, total, limit, lean):
    if count == 2:
        one = jax.random.randint(rng, (), max(1, total - limit), min(limit, total - 1) + 1)
        return jnp.stack([one, total - one])
    lengths = jnp.asarray(profile(count, total, limit, lean), jnp.int32)
    pairs = (count - 1) // 2
    source_of, receiver = lengths[1:1 + 2 * pairs:2], lengths[2:2 + 2 * pairs:2]
    room = jnp.minimum(source_of - 1, limit - receiver)
    passed = jax.random.randint(jax.random.fold_in(rng, 1), (pairs,), 0, 1 << 20) % (room + 1)
    lengths = lengths.at[1:1 + 2 * pairs:2].set(source_of - passed).at[2:2 + 2 * pairs:2].set(receiver + passed)
    return lengths[jax.random.permutation(jax.random.fold_in(rng, 2), count)]


def shared_out(stream_key, own, number, rows, count, top, bound, slope):
    sequence = jax.random.permutation(stream_key, count)
    crowded, common = shares(count, rows * top, bound, slope, True), shares(count, rows * top, bound, slope, False)
    places = jnp.arange(count)

    def named(sizes, offset_by):
        used = int((sizes > 0).sum())
        fixed = max(1, used // 4)
        shifted = fixed + (places - fixed + offset_by * (used - fixed)) % max(1, count - fixed)
        return jnp.zeros((count,), jnp.int32).at[sequence[jnp.where(places < fixed, places, shifted)]].set(jnp.asarray(sizes, jnp.int32))

    sizes = jnp.where(number % 4 == 0, named(crowded, number // 4), named(common, number - number // 4 - 1))
    mixed = jax.random.permutation(jax.random.fold_in(own, 3), count)
    source_of, taker = mixed[0:count // 2 * 2:2], mixed[1:count // 2 * 2:2]
    slack = jnp.minimum(sizes[source_of] - 1, bound - sizes[taker]) // 2
    slack = jnp.where((source_of == sequence[0]) | (taker == sequence[0]) | (sizes[taker] == 0), 0, jnp.maximum(slack, 0))
    shifted = jax.random.randint(jax.random.fold_in(own, 4), (count // 2,), 0, 1 << 20) % (slack + 1)
    sizes = sizes.at[source_of].add(-shifted).at[taker].add(shifted)
    items = jnp.searchsorted(jnp.cumsum(sizes), jnp.arange(rows * top), side="right").astype(jnp.int32)
    grid = items.reshape(top, rows).T
    grid = grid[jax.random.permutation(jax.random.fold_in(own, 1), rows)]
    offset_by = jax.random.randint(jax.random.fold_in(own, 2), (rows, 1), 0, top)
    return jnp.take_along_axis(grid, (jnp.arange(top)[None, :] + offset_by) % top, axis=1)


def shares(number_of, total, bound, slope, full):
    loads = [(1 << 20) // math.isqrt(rank ** slope) + 1 for rank in range(1, number_of + 1)]
    largest = bound if full else min(bound, max(-(-total // number_of), total * loads[0] // sum(loads)))
    least = 1 if total - largest >= number_of - 1 else 0
    counts, rest = [largest] + [least] * (number_of - 1), total - largest - least * (number_of - 1)
    while rest > 0:
        movable = [i for i in range(1, number_of) if counts[i] < largest] or [i for i in range(1, number_of) if counts[i] < bound]
        whole, budget = sum([loads[i] for i in movable]), rest
        for i in movable:
            extra = min(bound - counts[i], max(1, budget * loads[i] // whole), rest)
            counts[i] = counts[i] + extra
            rest = rest - extra
    return np.array(counts)


def scatter_about(own_key, dims, scale, most, split=(), kind=jnp.bfloat16):
    values = jax.random.normal(own_key, dims, jnp.float32) * scale
    if len(split) > 0:
        values = block_levels(own_key, dims, split, -0.22, 0.18) * values
    return jnp.clip(values, min=-most, max=most).astype(kind)


def gaussian_with(own_key, shape, scale, limit, shards, heavy, kind=jnp.bfloat16):
    drawn = scale * jax.random.normal(own_key, shape, jnp.float32)
    if shards:
        drawn = drawn * block_levels(own_key, shape, shards, -0.22, 0.18)
    return jnp.clip(raised(drawn, jax.random.fold_in(own_key, 3), *heavy), -limit, limit).astype(kind)


def setup_inputs(seed: int = 0) -> dict:
    seeds = jax.random.split(jax.random.key(seed), 11)
    tokens = scatter_about(seeds[0], (TOKENS, D), 1.0, 6.0, ((0, 32),))
    segments = jax.vmap(lambda own: jnp.searchsorted(jnp.cumsum(ragged_sizes(own, SEGS, LEN, LEN // 2, 0)), jnp.arange(LEN), side="right"))(jax.random.split(seeds[1], ROWS)).reshape((ROWS, LEN)).astype(jnp.int32)
    routes_keys = jax.random.split(jax.random.fold_in(seeds[2], 1), TOKENS // TOK_DEV)
    routes_turns = jax.random.permutation(jax.random.fold_in(seeds[2], 3), TOKENS // TOK_DEV)
    routes = jax.vmap(lambda own, number: shared_out(jax.random.fold_in(seeds[2], 2), own, number, TOK_DEV, 2, 1, MOST, 0))(routes_keys, routes_turns).reshape((TOKENS, 1))
    norm_gain = jnp.clip(1.0 + 0.15 * jax.random.normal(seeds[3], (LAYERS, 2, EXPERTS, D), jnp.float32), 0.25, 1.75).astype(jnp.bfloat16)
    norm_bias = scatter_about(seeds[4], (LAYERS, 2, EXPERTS, D), 0.3, 3.0, ((3, 8),))
    w_qkv = scatter_about(seeds[5], (LAYERS, D, 3 * D), D ** -0.5, 0.21875, ((1, 8),))
    w_out = scatter_about(seeds[6], (LAYERS, D, D), (D // 8) ** -0.5, 0.625, ((1, 8),))
    w_up = scatter_about(seeds[7], (LAYERS, EXPERTS, D, FF), D ** -0.5, 0.21875, ((2, 8),))
    w_down = scatter_about(seeds[8], (LAYERS, EXPERTS, FF, D), (FF // 2) ** -0.5, 0.15625, ((2, 8),))
    cotangent = gaussian_with(seeds[9], (TOKENS, D), 1.0, 6.0, ((0, 32),), (0, 1, 32, 2.75))
    return {"tokens": tokens, "segments": segments, "routes": routes, "norm_gain": norm_gain, "norm_bias": norm_bias, "w_qkv": w_qkv, "w_out": w_out, "w_up": w_up, "w_down": w_down, "cotangent": cotangent}


@jax.custom_vjp
def low(v):
    return lax.optimization_barrier(v.astype(jnp.bfloat16)).astype(jnp.float32)

@jax.custom_vjp
def low_back(v):
    return v

def low_keep(v):
    return (low(v), None)

def low_pass(kept, grad):
    return (grad,)

def back_keep(v):
    return (v, None)

def back_low(kept, grad):
    return (low(grad),)
low.defvjp(low_keep, low_pass)
low_back.defvjp(back_keep, back_low)
precise = lax.Precision.HIGHEST
far_below = -1e+30

def norm_rows(values, gain_rows, bias_rows):
    row_mean = lax.optimization_barrier(jnp.mean(values, axis=-1, keepdims=True))
    centred = values - row_mean
    spread = lax.optimization_barrier(jnp.mean(centred * centred, axis=-1, keepdims=True))
    return centred * lax.rsqrt(spread + 1e-05) * gain_rows + bias_rows

def attend_block(packed):
    qkv_rows, seg_rows = packed
    queries = qkv_rows[:, :, 0]
    keys_rows = qkv_rows[:, :, 1]
    values_rows = qkv_rows[:, :, 2]
    score_scale = HD ** (-0.5)
    scores = low_back(jnp.einsum('bqhd,bkhd->bhqk', queries, keys_rows, precision=precise) * score_scale)
    same_doc = seg_rows[:, None, :, None] == seg_rows[:, None, None, :]
    masked = jnp.where(same_doc, scores, far_below)
    row_top = lax.optimization_barrier(jnp.max(masked, axis=-1, keepdims=True))
    exponent = jnp.exp(masked - row_top)
    attn_prob = low(exponent / lax.optimization_barrier(jnp.sum(exponent, axis=-1, keepdims=True)))
    attn_out = jnp.einsum('bhqk,bkhd->bqhd', attn_prob, values_rows, precision=precise)
    return low(low_back(attn_out))

def one_layer(stream, layer_gain, layer_bias, qkv_weight, out_weight, up_weight, down_weight, second_route, segments):
    ref_rows = math.gcd(ROWS, max(1, 4096 // LEN))
    ffn_rows = math.gcd(TOKENS, 4096)
    first = low(norm_rows(stream, jnp.where(second_route, layer_gain[0, 1], layer_gain[0, 0]), jnp.where(second_route, layer_bias[0, 1], layer_bias[0, 0])))
    qkv_local = low(low_back(jnp.dot(first, qkv_weight, precision=precise)))
    qkv_blocks = qkv_local.reshape(ROWS // ref_rows, ref_rows, LEN, 3, H, HD)
    seg_blocks = segments.reshape(ROWS // ref_rows, ref_rows, LEN)
    attn = lax.map(jax.checkpoint(attend_block), (qkv_blocks, seg_blocks)).reshape(TOKENS, D)
    middle = stream + low_back(jnp.dot(attn, out_weight, precision=precise))
    second = low(norm_rows(middle, jnp.where(second_route, layer_gain[1, 1], layer_gain[1, 0]), jnp.where(second_route, layer_bias[1, 1], layer_bias[1, 0])))

    def expert_block(packed):
        block_rows, block_route = packed
        results = []
        for expert in range(EXPERTS):
            up_proj = low_back(jnp.dot(block_rows, up_weight[expert], precision=precise))
            active = low(jax.nn.gelu(up_proj, approximate=False))
            results.append(jnp.dot(active, down_weight[expert], precision=precise))
        return low_back(jnp.where(block_route, results[1], results[0]))
    branch = lax.map(jax.checkpoint(expert_block), (second.reshape(TOKENS // ffn_rows, ffn_rows, D), second_route.reshape(TOKENS // ffn_rows, ffn_rows, 1))).reshape(TOKENS, D)
    return middle + branch

def reference(tokens, segments, routes, norm_gain, norm_bias, w_qkv, w_out, w_up, w_down, cotangent):
    second_route = routes == 1

    def forward(stream, gain_all, bias_all, qkv_all, out_all, up_all, down_all):
        for layer in range(LAYERS):
            stream = one_layer(stream, gain_all[layer], bias_all[layer], qkv_all[layer], out_all[layer], up_all[layer], down_all[layer], second_route, segments)
        return stream
    output, pull = jax.vjp(forward, tokens.astype(jnp.float32), norm_gain.astype(jnp.float32), norm_bias.astype(jnp.float32), w_qkv.astype(jnp.float32), w_out.astype(jnp.float32), w_up.astype(jnp.float32), w_down.astype(jnp.float32))
    grads = pull(cotangent.astype(jnp.float32))
    return (output, grads[0], grads[1], grads[2], grads[3], grads[4], grads[5], grads[6])
```

```python
import jax
import jax.numpy as jnp
from jax import lax
from jax.experimental import pallas as pl
from jax.experimental.pallas import tpu as pltpu
from jax.sharding import PartitionSpec as P

H = 12
HD = 64
BF = jnp.bfloat16
F32 = jnp.float32
VMEM_BYTES = 26 * 1024 * 1024
COLS = 256
PACKED = 768
KEPT = 640

far_below = -1e30
scale = HD**-0.5


def nn(a, b):
    return lax.dot_general(a, b, (((1,), (0,)), ((), ())), preferred_element_type=F32)


def nt(a, b):
    return lax.dot_general(a, b, (((1,), (1,)), ((), ())), preferred_element_type=F32)


def tn(a, b):
    return lax.dot_general(a, b, (((0,), (0,)), ((), ())), preferred_element_type=F32)


def shape(*dims, dtype=BF):
    return jax.ShapeDtypeStruct(dims, dtype)


def smem():
    return pl.BlockSpec(memory_space=pltpu.SMEM)


def whole(*dims):
    return pl.BlockSpec(dims, lambda i: (0,) * len(dims))


def call(kernel, out_shape, name, micros=0, **rest):
    return pl.pallas_call(
        kernel,
        out_shape=out_shape,
        name=name,
        compiler_params=pltpu.CompilerParams(vmem_limit_bytes=VMEM_BYTES),
        cost_estimate=pl.CostEstimate(
            flops=micros * 1_000_000_000, bytes_accessed=0, transcendentals=0
        ),
        **rest,
    )


def unit_of(values):
    centred = values - jnp.mean(values, axis=-1, keepdims=True)
    inv_std = lax.rsqrt(jnp.mean(centred * centred, axis=-1, keepdims=True) + 1e-05)
    return centred * inv_std, inv_std


def norm_rows(values, par_ref, second):
    gain = jnp.where(second, par_ref[1:2, :], par_ref[0:1, :])
    bias = jnp.where(second, par_ref[3:4, :], par_ref[2:3, :])
    return (unit_of(values)[0] * gain + bias).astype(BF)


def norm_back_rows(grad, incoming, base, par_ref, second, terms_ref):
    unit, inv_std = unit_of(base)
    scaled = incoming * jnp.where(second, par_ref[1:2, :], par_ref[0:1, :])
    fresh = grad + inv_std * (
        scaled
        - jnp.mean(scaled, axis=-1, keepdims=True)
        - unit * jnp.mean(scaled * unit, axis=-1, keepdims=True)
    )
    gain_term = incoming * unit
    zero = jnp.zeros_like(incoming)
    terms_ref[0:1, :] += jnp.sum(jnp.where(second, zero, gain_term), axis=0, keepdims=True)
    terms_ref[1:2, :] += jnp.sum(jnp.where(second, gain_term, zero), axis=0, keepdims=True)
    terms_ref[2:3, :] += jnp.sum(jnp.where(second, zero, incoming), axis=0, keepdims=True)
    terms_ref[3:4, :] += jnp.sum(jnp.where(second, incoming, zero), axis=0, keepdims=True)
    return fresh


def each_block(head, mine_ref, other_ref, act):
    core = head & 1
    pairs, rows = mine_ref.shape[0], mine_ref.shape[1]
    for pair in range(pairs):
        for ref, side in ((mine_ref, core), (other_ref, 1 - core)):
            at = pl.multiple_of((2 * pair + side) * rows, rows)
            act(pl.ds(at, rows), ref[pair].astype(F32))


def split_out(head, total_ref, keep_ref, send_ref):
    core = head & 1
    pairs, rows = keep_ref.shape[0], keep_ref.shape[1]
    for pair in range(pairs):
        at = pl.multiple_of((2 * pair + core) * rows, rows)
        keep_ref[pair] = total_ref[pl.ds(at, rows), :]
        at = pl.multiple_of((2 * pair + 1 - core) * rows, rows)
        send_ref[pair] = total_ref[pl.ds(at, rows), :].astype(BF)


def attend_math(first_ref, w_ref, segc_ref, segr_ref, qkv_ref, attn_ref, lse_ref):
    heads = attn_ref.shape[0] // HD
    qkv = nn(first_ref[...], w_ref[:, : qkv_ref.shape[1]]).astype(BF)
    qkv_ref[...] = qkv
    turned = qkv.T
    same = segc_ref[...] == segr_ref[...]
    for j in range(heads):
        at_q, at_k, at_v = (HD * (j + heads * part) for part in range(3))
        scores = nn(qkv[:, at_k : at_k + HD], turned[at_q : at_q + HD]) * scale
        scores = jnp.where(same, scores, far_below)
        top = jnp.max(scores, axis=0, keepdims=True)
        exponent = jnp.exp(scores - top)
        total = jnp.sum(exponent, axis=0, keepdims=True)
        prob = (exponent / total).astype(BF)
        attn_ref[HD * j : HD * (j + 1), :] = nn(turned[at_v : at_v + HD], prob).astype(BF)
        lse_ref[j : j + 1, :] = top + jnp.log(total)


def join_lanes(blocks_ref, layer, out_ref):
    cols = out_ref.shape[1] // blocks_ref.shape[0]
    for part in range(blocks_ref.shape[0]):
        out_ref[:, part * cols : (part + 1) * cols] = blocks_ref[
            part, :, layer * cols : (layer + 1) * cols
        ]


def attend_first_kernel(
    tok_ref, small_ref, route_ref, w_ref, segc_ref, segr_ref,
    par_ref, first_ref, qkv_ref, attn_ref, lse_ref,
):
    turned = small_ref[...].astype(F32).T
    par_ref[...] = turned[: par_ref.shape[0]]
    first_ref[...] = norm_rows(tok_ref[...].astype(F32), par_ref, route_ref[...] == 1)
    attend_math(first_ref, w_ref, segc_ref, segr_ref, qkv_ref, attn_ref, lse_ref)


def project_kernel(head_ref, attn_ref, wo_ref, keep_ref, send_ref, total_ref, wide_ref):
    join_lanes(wo_ref, 0, wide_ref)
    total_ref[...] = tn(attn_ref[...], wide_ref[...])
    split_out(head_ref[0], total_ref, keep_ref, send_ref)


def attend_kernel(
    layer, head_ref, base_ref, mine_ref, other_ref, par_ref, route_ref, w_ref, wo_ref, segc_ref, segr_ref,
    stream_ref, first_ref, qkv_ref, attn_ref, lse_ref, keep_ref, send_ref, total_ref, wide_ref,
):
    def act(rows, fresh):
        values = base_ref[rows, :].astype(F32) + fresh
        stream_ref[rows, :] = values
        first_ref[rows, :] = norm_rows(values, par_ref, route_ref[rows, :] == 1)

    each_block(head_ref[0], mine_ref, other_ref, act)
    attend_math(first_ref, w_ref, segc_ref, segr_ref, qkv_ref, attn_ref, lse_ref)
    join_lanes(wo_ref, layer, wide_ref)
    total_ref[...] = tn(attn_ref[...], wide_ref[...])
    split_out(head_ref[0], total_ref, keep_ref, send_ref)


def split_sides(dp_ref, bit, grads_ref, send_ref, keep_ref):
    side = (dp_ref[0] >> bit) & 1
    rows = send_ref.shape[-2]
    for out_ref, flip in ((send_ref, 1), (keep_ref, 0)):
        for place in range(out_ref.shape[0]):
            low = place % (1 << bit)
            block = ((place - low) << 1) + low + ((side ^ flip) << bit)
            at = pl.ds(pl.multiple_of(block * rows, 16), rows)
            if len(out_ref.shape) == 3:
                out_ref[place] = grads_ref[at, :]
            else:
                for member in range(out_ref.shape[1]):
                    out_ref[place, member] = grads_ref[member, at, :]


def attend_back_kernel(
    layer, head_ref, grad_ref, mine_ref, other_ref, base_ref, par_ref, route_ref,
    qkv_ref, lse_ref, w_ref, wo_ref, segc_ref, segr_ref,
    fresh_ref, terms_ref, m_ref, gqkv_ref, keep_ref, send_ref, total_ref, turned_ref, wide_ref,
):
    terms_ref[...] = jnp.zeros_like(terms_ref)

    def act(rows, incoming):
        fresh = norm_back_rows(
            grad_ref[rows, :].astype(F32), incoming, base_ref[rows, :].astype(F32),
            par_ref, route_ref[rows, :] == 1, terms_ref,
        )
        fresh_ref[rows, :] = fresh
        m_ref[rows, :] = fresh.astype(BF)

    each_block(head_ref[0], mine_ref, other_ref, act)
    join_lanes(wo_ref, layer, wide_ref)
    heads = wide_ref.shape[0] // HD
    grad_attn = nt(wide_ref[...], m_ref[...]).astype(BF)
    qkv = qkv_ref[...]
    turned = qkv.T
    same = segc_ref[...] == segr_ref[...]
    for j in range(heads):
        at_q, at_k, at_v = (HD * (j + heads * part) for part in range(3))
        scores = nn(qkv[:, at_k : at_k + HD], turned[at_q : at_q + HD]) * scale
        prob = jnp.exp(jnp.where(same, scores, far_below) - lse_ref[j : j + 1, :])
        g_out = grad_attn[HD * j : HD * (j + 1)]
        g_prob = nn(qkv[:, at_v : at_v + HD], g_out)
        inner = jnp.sum(prob * g_prob, axis=0, keepdims=True)
        g_scores = (prob * (g_prob - inner)).astype(BF)
        g_q = nn(turned[at_k : at_k + HD], g_scores) * scale
        g_k = nt(turned[at_q : at_q + HD], g_scores) * scale
        g_v = nt(g_out, prob.astype(BF))
        turned_ref[at_q : at_q + HD, :] = g_q.astype(BF)
        turned_ref[at_k : at_k + HD, :] = g_k.astype(BF)
        turned_ref[at_v : at_v + HD, :] = g_v.astype(BF)
    used = 3 * heads * HD
    turned_ref[used:, :] = jnp.zeros((turned_ref.shape[0] - used, turned_ref.shape[1]), BF)
    g_qkv = turned_ref[...].T
    gqkv_ref[...] = g_qkv
    total_ref[...] = nt(g_qkv, w_ref[:, : g_qkv.shape[1]])
    split_out(head_ref[0], total_ref, keep_ref, send_ref)


def attend_grads_kernel(
    head_ref, dp_ref, first_ref, gqkv_ref, attn_ref, m_ref, after_ref, *rest
):
    zero_ref, *gw_refs, grads_ref = rest
    zero_ref[0, 0] = 0.0
    into_ref = gw_refs[0] if len(gw_refs) == 1 else grads_ref
    cols = into_ref.shape[1] // 4
    grads = tn(first_ref[...], gqkv_ref[...]).astype(BF)
    into_ref[:, : 3 * cols] = grads[:, : 3 * cols]
    for j in range(4):

        @pl.when(head_ref[0] == j)
        def _():
            into_ref[:, 3 * cols :] = nn(
                attn_ref[0], m_ref[:, j * cols : (j + 1) * cols]
            ).astype(BF)

    if len(gw_refs) > 1:
        split_sides(dp_ref, 0, grads_ref, *gw_refs)


def add_up(term, total_ref):
    step = pl.program_id(0)

    @pl.when(step == 0)
    def _():
        total_ref[...] = term

    @pl.when(step > 0)
    def _():
        total_ref[...] += term


def feed_kernel(
    head_ref, base_ref, mine_ref, other_ref, par_ref, route_ref, wu0_ref, wu1_ref, wd0_ref, wd1_ref,
    middle_ref, x_ref, act_ref, slope_ref, keep_ref, send_ref, total_ref,
):
    step = pl.program_id(0)

    @pl.when(step == 0)
    def _():
        def act(rows, fresh):
            values = base_ref[rows, :].astype(F32) + fresh
            middle_ref[rows, :] = values
            x_ref[rows, :] = norm_rows(values, par_ref, route_ref[rows, :] == 1)

        each_block(head_ref[0], mine_ref, other_ref, act)

    second = route_ref[...] == 1
    x = x_ref[...]
    up = jnp.where(second, nn(x, wu1_ref[...]), nn(x, wu0_ref[...]))
    phi = 0.5 * (1.0 + lax.erf(up * 0.7071067811865476))
    active = (up * phi).astype(BF)
    act_ref[...] = active
    slope_ref[...] = (phi + up * jnp.exp(-0.5 * up * up) * 0.3989422804014327).astype(BF)
    zero = jnp.zeros_like(active)
    term = nn(jnp.where(second, zero, active), wd0_ref[...])
    term += nn(jnp.where(second, active, zero), wd1_ref[...])
    add_up(term, total_ref)

    @pl.when(step == pl.num_programs(0) - 1)
    def _():
        split_out(head_ref[0], total_ref, keep_ref, send_ref)


def feed_back_math(
    head_ref, g_ref, slope_ref, wu0_ref, wu1_ref, wd0_ref, wd1_ref, route_ref,
    gup_ref, keep_ref, send_ref, total_ref,
):
    second = route_ref[...] == 1
    g_b = g_ref[...]
    g_up = jnp.where(second, nt(g_b, wd1_ref[...]), nt(g_b, wd0_ref[...]))
    g_up = (g_up * slope_ref[...].astype(F32)).astype(BF)
    gup_ref[...] = g_up
    zero = jnp.zeros_like(g_up)
    term = nt(jnp.where(second, zero, g_up), wu0_ref[...])
    term += nt(jnp.where(second, g_up, zero), wu1_ref[...])
    add_up(term, total_ref)

    @pl.when(pl.program_id(0) == pl.num_programs(0) - 1)
    def _():
        split_out(head_ref[0], total_ref, keep_ref, send_ref)


def feed_back_first_kernel(
    head_ref, g_ref, slope_ref, wu0_ref, wu1_ref, wd0_ref, wd1_ref, route_ref,
    gup_ref, keep_ref, send_ref, total_ref,
):
    feed_back_math(
        head_ref, g_ref, slope_ref, wu0_ref, wu1_ref, wd0_ref, wd1_ref, route_ref,
        gup_ref, keep_ref, send_ref, total_ref,
    )


def feed_back_kernel(
    head_ref, grad_ref, mine_ref, other_ref, base_ref, par_ref,
    slope_ref, wu0_ref, wu1_ref, wd0_ref, wd1_ref, route_ref,
    fresh_ref, terms_ref, g_ref, gup_ref, keep_ref, send_ref, total_ref,
):
    @pl.when(pl.program_id(0) == 0)
    def _():
        terms_ref[...] = jnp.zeros_like(terms_ref)

        def act(rows, incoming):
            fresh = norm_back_rows(
                grad_ref[rows, :], incoming, base_ref[rows, :],
                par_ref, route_ref[rows, :] == 1, terms_ref,
            )
            fresh_ref[rows, :] = fresh
            g_ref[rows, :] = fresh.astype(BF)

        each_block(head_ref[0], mine_ref, other_ref, act)

    feed_back_math(
        head_ref, g_ref, slope_ref, wu0_ref, wu1_ref, wd0_ref, wd1_ref, route_ref,
        gup_ref, keep_ref, send_ref, total_ref,
    )


def feed_grads_kernel(
    carried, dp_ref, g_ref, x_ref, act_ref, gup_ref, route_ref, after_ref, attn_ref, *rest
):
    above, (zero_ref, *outs, turned_ref, grads_ref) = rest[:carried], rest[carried:]
    zero_ref[0, 0] = 0.0
    step = pl.program_id(0)
    cols = act_ref.shape[1]
    second = route_ref[...] == 1

    @pl.when(step == 0)
    def _():
        turned_ref[...] = x_ref[...].T

    into_ref = outs[0] if len(outs) == 1 else grads_ref
    active = act_ref[...]
    g_up = gup_ref[...]
    zero = jnp.zeros_like(g_up)
    here = pl.ds(pl.multiple_of(step * cols, cols), cols)
    for expert in range(2):
        mine = second if expert else jnp.logical_not(second)
        into_ref[expert, :, here] = nn(turned_ref[...], jnp.where(mine, g_up, zero)).astype(BF)
        into_ref[2 + expert, here, :] = tn(jnp.where(mine, active, zero), g_ref[...]).astype(BF)

    @pl.when(step == pl.num_programs(0) - 1)
    def _():
        if len(outs) > 1:
            split_sides(dp_ref, 0, grads_ref.at[:2], outs[0].at[:, :2], outs[1].at[:, :2])
            for from_ref, to_ref in zip(above, outs):
                to_ref[:, 2] = from_ref[...]
            split_sides(dp_ref, 1, grads_ref.at[2:], outs[2], outs[3])


def last_add_kernel(head_ref, middle_ref, own_ref, recv_ref, out_ref):
    rows = out_ref.shape[0]
    at = pl.multiple_of(head_ref[0] * rows, rows)
    out_ref[...] = middle_ref[pl.ds(at, rows), :] + own_ref[...] + recv_ref[...].astype(F32)


def last_norm_kernel(head_ref, grad_ref, own_ref, recv_ref, tok_ref, par_ref, route_ref, *refs):
    out_ref, terms_ref = refs[-2:]
    terms_ref[...] = jnp.zeros_like(terms_ref)
    rows = out_ref.shape[0]
    at = pl.multiple_of(head_ref[0] * rows, rows)
    out_ref[...] = norm_back_rows(
        grad_ref[pl.ds(at, rows), :], own_ref[...] + recv_ref[...].astype(F32),
        tok_ref[...].astype(F32), par_ref, route_ref[...] == 1, terms_ref,
    )


def add_split_kernel(count, bit, dp_ref, *refs):
    inputs, (send_ref, keep_ref) = refs[:count], refs[-2:]
    side = (dp_ref[0] >> bit) & 1
    for out_ref, flip in ((send_ref, 1), (keep_ref, 0)):
        for place in range(out_ref.shape[0]):
            at = 2 * place + (side ^ flip)
            lane = 0
            for one_ref, two_ref in zip(inputs[::2], inputs[1::2]):
                cols = one_ref.shape[-1]
                total = (one_ref[at].astype(F32) + two_ref[at].astype(F32)).astype(BF)
                out_ref[place, ..., lane : lane + cols] = total
                lane += cols


def add_last_kernel(count, *refs):
    inputs, out_ref = refs[:count], refs[-1]
    lane = 0
    for one_ref, two_ref in zip(inputs[::2], inputs[1::2]):
        cols = one_ref.shape[-1]
        total = (one_ref[0].astype(F32) + two_ref[0].astype(F32)).astype(BF)
        out_ref[..., lane : lane + cols] = total
        lane += cols


def add_each_kernel(count, *refs):
    for group in range(count):
        one_ref, two_ref = refs[2 * group : 2 * group + 2]
        total = one_ref[0].astype(F32) + two_ref[0].astype(F32)
        refs[group - count][...] = total.astype(BF)


def tie_kernel(array_ref, after_ref, out_ref):
    pass


def pack_kernel(head_ref, up_ref, down_ref, *refs):
    out_ref, tall_ref = refs[-2:]
    width = down_ref.shape[3]
    count = 4
    hidden = up_ref.shape[3] // count
    sub = down_ref.shape[2] // count
    for j in range(count):

        @pl.when(head_ref[0] == j)
        def _():
            for expert in range(2):
                to = (2 + expert) * hidden
                out_ref[:, to : to + width] = down_ref[0, expert, j * sub : (j + 1) * sub, :]
                for block in range(hidden // sub):
                    at = block * sub * count + j * sub
                    to = expert * hidden + block * sub
                    out_ref[:, to : to + sub] = up_ref[0, expert, :, at : at + sub]
            if out_ref.shape[1] > 4 * hidden:
                qkv_ref, wo_ref, small_ref = refs[:3]
                cols = width // count
                for layer in range(qkv_ref.shape[0]):
                    to = 4 * hidden + layer * PACKED
                    for part in range(3):
                        at = part * width + j * cols
                        out_ref[:, to : to + cols] = qkv_ref[layer, :, at : at + cols]
                        to += cols
                    out_ref[:, to : to + cols] = wo_ref[layer, :, j * cols : (j + 1) * cols]
                tall_ref[...] = jnp.zeros_like(tall_ref)
                tall_ref[: small_ref.shape[0], : small_ref.shape[1]] = small_ref[...].astype(F32)
                out_ref[:, 4 * hidden + qkv_ref.shape[0] * PACKED :] = tall_ref[...].T[
                    : out_ref.shape[0]
                ].astype(BF)


def gather_refs(head_ref, arrays, blocks_ref):
    for s in range(4):
        blocks_ref[head_ref[0] ^ s] = arrays[s][...]


def unpack_up(blocks_ref, gu_ref):
    sub = blocks_ref.shape[2]
    for h in range(4):
        for expert in range(2):
            for block in range(gu_ref.shape[3] // (4 * sub)):
                at = block * 4 * sub + h * sub
                gu_ref[0, expert, :, at : at + sub] = blocks_ref[
                    h, expert, :, block * sub : (block + 1) * sub
                ].astype(F32)


def unpack_down(blocks_ref, first, gd_ref):
    sub = blocks_ref.shape[2]
    for h in range(4):
        for expert in range(2):
            gd_ref[0, expert, h * sub : (h + 1) * sub, :] = blocks_ref[h, first + expert].astype(F32)


def unpack_qkv(block_of, gq_ref, go_ref):
    cols = go_ref.shape[2] // 4
    for h in range(4):
        for part in range(3):
            to = part * 4 * cols + h * cols
            gq_ref[0, :, to : to + cols] = block_of(h, part * cols, cols).astype(F32)
        go_ref[0, :, h * cols : (h + 1) * cols] = block_of(h, 3 * cols, cols).astype(F32)


def unpack_later_kernel(head_ref, ffn_ref, gu_ref, gd_ref):
    unpack_up(ffn_ref, gu_ref)
    unpack_down(ffn_ref, 2, gd_ref)


def unpack_up_kernel(head_ref, *refs):
    gu_ref, gq_ref, go_ref, blocks_ref = refs[-4:]
    gather_refs(head_ref, refs[:4], blocks_ref)
    unpack_up(blocks_ref, gu_ref)
    unpack_qkv(lambda h, at, cols: blocks_ref[h, 2, :, at : at + cols], gq_ref, go_ref)


def unpack_down_kernel(head_ref, blocks_ref, *refs):
    unpack_down(blocks_ref, 0, refs[-1])


def unpack_attn_kernel(head_ref, *refs):
    gq_ref, go_ref, gain_ref, bias_ref, blocks_ref = refs[-5:]
    gather_refs(head_ref, refs[:4], blocks_ref)
    unpack_qkv(lambda h, at, cols: blocks_ref[h, :, 128 + at : 128 + at + cols], gq_ref, go_ref)
    terms = blocks_ref[0, :, :128].astype(F32)
    for h in range(1, 4):
        terms += blocks_ref[h, :, :128].astype(F32)
    turned = terms.T
    for layer in range(2):
        for place in range(2):
            at = 8 * layer + 4 * place
            gain_ref[layer, place] = turned[at : at + 2]
            bias_ref[layer, place] = turned[at + 2 : at + 4]


def swap(array, axis, bits):
    count = lax.axis_size(axis)
    return lax.ppermute(array, axis, [(i, i ^ bits) for i in range(count)])


def half_sum(keep, send):
    return (keep + swap(send, "head", 1).astype(F32)).astype(BF)


def other_half(half, zero=None):
    recv = swap(half, "head", 2).astype(F32)
    if zero is not None:
        recv = recv + zero.reshape(())
    mine = (half.astype(F32) + recv).astype(BF)
    return mine, swap(mine, "head", 1)


def head_sum(keep, send):
    return other_half(half_sum(keep, send))


def own_sum(half, head_at):
    pair = head_at // 2
    recv = swap(lax.dynamic_index_in_dim(half, 1 - pair, 0, keepdims=False).astype(BF), "head", 2)
    return lax.dynamic_index_in_dim(half, pair, 0, keepdims=False), recv


def spread(array, axis):
    copies = jnp.broadcast_to(array[None], (lax.axis_size(axis),) + array.shape)
    return lax.all_to_all(copies, axis, 0, 0, tiled=True)


def head_pieces(shard):
    across = swap(shard, "head", 2)
    return [shard, swap(shard, "head", 1), across, swap(across, "head", 1)]


def by_pairs(grads, dp_at, dp_count):
    sides = grads.reshape(dp_count // 2, 2, -1, grads.shape[-1])
    side = dp_at % 2
    return (
        lax.dynamic_index_in_dim(sides, 1 - side, 1, keepdims=False),
        lax.dynamic_index_in_dim(sides, side, 1, keepdims=False),
    )


def add_split(dp_index, lists, bit, after):
    flat = [array for pair in lists for array in pair]
    lanes = sum(keep.shape[-1] for keep, _ in lists)
    dims = (flat[0].shape[0] // 2,) + flat[0].shape[1:-1] + (lanes,)
    vmem = pl.BlockSpec(memory_space=pltpu.VMEM)
    send, keep = call(
        lambda *refs: add_split_kernel(len(flat), bit, *refs), (shape(*dims),) * 2, "add_split",
        in_specs=[smem()] + [vmem] * len(flat) + [pl.BlockSpec(memory_space=pl.ANY)] * len(after),
    )(dp_index, *flat, *after)
    return [(keep, swap(send, "dp", 1 << bit))]


def add_last(lists, after=()):
    flat = [array for pair in lists for array in pair]
    lanes = sum(keep.shape[-1] for keep, _ in lists)
    vmem = pl.BlockSpec(memory_space=pltpu.VMEM)
    return call(
        lambda *refs: add_last_kernel(len(flat), *refs),
        shape(*flat[0].shape[1:-1], lanes), "add_last",
        in_specs=[vmem] * len(flat) + [pl.BlockSpec(memory_space=pl.ANY)] * len(after),
    )(*flat, *after)


def add_each(groups, after):
    flat = [array for pair in groups for array in pair]
    vmem = pl.BlockSpec(memory_space=pltpu.VMEM)
    return call(
        lambda *refs: add_each_kernel(len(groups), *refs),
        [shape(*keep.shape[1:]) for keep, _ in groups], "add_each",
        in_specs=[vmem] * len(flat) + [pl.BlockSpec(memory_space=pl.ANY)] * len(after),
    )(*flat, *after)


def tie(array, after):
    return call(
        tie_kernel, shape(*array.shape), "tie",
        in_specs=[pl.BlockSpec(memory_space=pl.ANY)] * 2,
        out_specs=pl.BlockSpec(memory_space=pl.ANY),
        input_output_aliases={0: 0},
    )(array, after)


def body(tokens, segments, routes, norm_gain, norm_bias, w_qkv, w_out, w_up, w_down, cotangent):
    dp_count = lax.axis_size("dp")
    head_count = lax.axis_size("head")
    head_at = lax.axis_index("head")
    dp_at = lax.axis_index("dp")
    head = head_at.reshape(1)
    dp_index = dp_at.reshape(1)
    tok_count, width = tokens.shape
    row_len = segments.shape[1]
    layers = norm_gain.shape[0]
    head_cols = H // head_count * HD
    hidden_all = w_up.shape[3]
    hidden = hidden_all // head_count
    rows = w_qkv.shape[1]
    down_rows = w_down.shape[2]
    sub = down_rows // head_count
    steps = hidden // COLS
    aligned = rows % 16 == 0 and dp_count == 8 and head_count == 4 and layers == 2

    small = jnp.stack([norm_gain, norm_bias], axis=2).reshape(layers * 8, rows)

    seg_col = segments.reshape(row_len, 1)
    seg_row = segments.reshape(1, row_len)
    route_lanes = jnp.pad(routes.astype(BF), ((0, 0), (0, 127)))
    both = spread(jnp.concatenate([tokens, cotangent, route_lanes], axis=1), "head")
    both = both.reshape(row_len, 2 * width + 128)
    row_tokens = both[:, :width]
    row_cotangent = both[:, width : 2 * width]
    row_routes = both[:, 2 * width : 2 * width + 1].astype(jnp.int32)

    packs = []
    for layer in range(layers):
        extra = (w_qkv, w_out, small) if layer == 0 else ()
        first = (row_tokens, row_cotangent, row_routes) if layer else ()
        lanes = 4 * width + (0 if layer else layers * PACKED + 128)
        if aligned:
            packs.append(
                call(
                    pack_kernel,
                    shape(rows, lanes),
                    "pack",
                    grid=(1,),
                    in_specs=[
                        smem(),
                        pl.BlockSpec(
                            (1, 2, rows, hidden_all), lambda i, layer=layer: (layer, 0, 0, 0)
                        ),
                        pl.BlockSpec(
                            (1, 2, down_rows, width), lambda i, layer=layer: (layer, 0, 0, 0)
                        ),
                    ]
                    + [whole(*array.shape) for array in extra]
                    + [pl.BlockSpec(memory_space=pl.ANY)] * len(first),
                    out_specs=whole(rows, lanes),
                    scratch_shapes=[pltpu.VMEM((128, 128), F32)],
                )(head, w_up, w_down, *extra, *first)
            )
        else:
            taken = lax.dynamic_index_in_dim(
                w_up[layer].reshape(2, rows, dp_count, head_count, sub), head_at, 3, keepdims=False
            ).reshape(2, rows, hidden)
            down = lax.dynamic_index_in_dim(
                w_down[layer].reshape(2, head_count, sub, width), head_at, 1, keepdims=False
            )
            parts = [taken[0], taken[1], down[0], down[1]]
            for at in range(layers if layer == 0 else 0):
                taken = lax.dynamic_index_in_dim(
                    w_qkv[at].reshape(rows, 3, head_count, head_cols), head_at, 2, keepdims=False
                )
                out = lax.dynamic_index_in_dim(
                    w_out[at].reshape(rows, head_count, head_cols), head_at, 1, keepdims=False
                )
                parts += [taken.reshape(rows, 3 * head_cols), out]
            if layer == 0:
                parts.append(jnp.pad(small.T, ((0, 0), (0, 128 - layers * 8))))
            packs.append(jnp.concatenate(parts, axis=1))
    gathered = [lax.all_gather(pack, "dp", axis=0, tiled=True) for pack in packs]
    taken = [
        gathered[0][:, at : at + head_cols]
        for at in (4 * width + layer * PACKED + 3 * head_cols for layer in range(layers))
    ]
    out_w = lax.all_to_all(
        jnp.concatenate(taken, axis=1).reshape(head_count, head_cols, layers * head_cols),
        "head", 0, 0, tiled=True,
    )

    pairs = head_count // 2
    flat = (row_len, width)
    halves = (pairs, tok_count, width)
    both_halves = (shape(*halves, dtype=F32), shape(*halves))
    half_specs = [whole(*halves), whole(*halves)]
    per_expert = width // COLS
    weight_specs = [
        pl.BlockSpec((width, COLS), lambda i: (0, i)),
        pl.BlockSpec((width, COLS), lambda i: (0, per_expert + i)),
        pl.BlockSpec((COLS, width), lambda i: (i, 2)),
        pl.BlockSpec((COLS, width), lambda i: (i, 3)),
    ]
    act_spec = pl.BlockSpec((row_len, COLS), lambda i: (0, i))
    total = pltpu.VMEM(flat, F32)
    vmem = pl.BlockSpec(memory_space=pltpu.VMEM)

    def attn_spec(layer):
        return pl.BlockSpec((width, PACKED), lambda i: (0, 4 * width // PACKED + layer))

    small_spec = pl.BlockSpec((width, 128), lambda i: (0, 4 * width // 128 + layers * PACKED // 128))
    out_spec = whole(head_count, head_cols, layers * head_cols)
    seg_specs = [whole(row_len, 1), whole(1, row_len)]
    wide = pltpu.VMEM((head_cols, width), BF)

    saved = []
    for layer in range(layers):
        kept = (
            shape(*flat), shape(row_len, KEPT), shape(head_cols, row_len),
            shape(8, row_len, dtype=F32),
        )
        kept_specs = [whole(*array.shape) for array in kept]
        if layer == 0:
            stream = row_tokens
            pars, first, qkv, attn, lse = call(
                attend_first_kernel, (shape(layers * 8, width, dtype=F32),) + kept, "attend_first",
                grid=(1,),
                in_specs=[whole(*flat), small_spec, whole(row_len, 1), attn_spec(0)] + seg_specs,
                out_specs=[whole(layers * 8, width)] + kept_specs,
            )(stream, gathered[0], row_routes, gathered[0], seg_col, seg_row)
            pars = pars.reshape(layers, 2, 4, width)
            keep, send = call(
                project_kernel, both_halves, "project",
                in_specs=[smem()] + [vmem] * 2,
                scratch_shapes=[total, wide],
            )(head, attn, out_w)
        else:
            stream, first, qkv, attn, lse, keep, send = call(
                lambda *refs, layer=layer: attend_kernel(layer, *refs),
                (shape(*flat, dtype=F32),) + kept + both_halves,
                "attend",
                grid=(1,),
                in_specs=[smem(), whole(*flat)] + half_specs
                + [whole(4, width), whole(row_len, 1), attn_spec(layer), out_spec] + seg_specs,
                out_specs=[whole(*flat)] + kept_specs + half_specs,
                scratch_shapes=[total, wide],
            )(
                head, middle, mine, other, pars[layer, 0], row_routes, gathered[0], out_w,
                seg_col, seg_row,
            )
        mine, other = head_sum(keep, send)
        middle, second, active, slope, keep, send = call(
            feed_kernel,
            (shape(*flat, dtype=F32), shape(*flat), shape(row_len, hidden), shape(row_len, hidden))
            + both_halves,
            "feed",
            grid=(steps,),
            in_specs=[smem(), whole(*flat)] + half_specs
            + [whole(4, width), whole(row_len, 1)] + weight_specs,
            out_specs=[whole(*flat), whole(*flat), act_spec, act_spec] + half_specs,
            scratch_shapes=[total],
        )(head, stream, mine, other, pars[layer, 1], row_routes, *[gathered[layer]] * 4)
        saved.append((stream, first, qkv, attn, lse, middle, second, active, slope))
        if layer + 1 < layers:
            mine, other = head_sum(keep, send)
    half = keep + swap(send, "head", 1).astype(F32)
    attn_all = lax.all_gather(
        jnp.stack([entry[3] for entry in saved]), "head", axis=1, tiled=True
    )
    own, recv = own_sum(half, head_at)
    output = call(
        last_add_kernel, shape(tok_count, width, dtype=F32), "last_add",
        in_specs=[smem()] + [vmem] * 3,
    )(head, middle, own, recv)

    term_list = [None] * (2 * layers)
    ffn_shards = [None] * layers
    attn_grads = [None] * layers
    markers = {}
    fresh_terms = (shape(*flat, dtype=F32), shape(8, width, dtype=F32))
    whole_grads = (4, width, hidden)
    chunk = (dp_count // 2, 2, rows, width)
    narrow = (dp_count // 2, rows, width)
    gradient = row_cotangent
    for layer in reversed(range(layers)):
        stream, first, qkv, attn, lse, middle, second, active, slope = saved[layer]
        operands = (slope,) + (gathered[layer],) * 4 + (row_routes,)
        operand_specs = [act_spec] + weight_specs + [whole(row_len, 1)]
        if layer == layers - 1:
            grad_b = gradient
            g_up, keep, send = call(
                feed_back_first_kernel, (shape(row_len, hidden),) + both_halves,
                "feed_back_first",
                grid=(steps,),
                in_specs=[smem(), whole(*flat)] + operand_specs,
                out_specs=[act_spec] + half_specs,
                scratch_shapes=[total],
            )(head, gradient, *operands)
        else:
            gradient, terms, grad_b, g_up, keep, send = call(
                feed_back_kernel,
                fresh_terms + (shape(*flat), shape(row_len, hidden)) + both_halves,
                "feed_back",
                grid=(steps,),
                in_specs=[smem(), whole(*flat)] + half_specs
                + [whole(*flat), whole(4, width)] + operand_specs,
                out_specs=[whole(*flat), whole(8, width), whole(*flat), act_spec] + half_specs,
                scratch_shapes=[total],
            )(
                head, gradient, mine, other, saved[layer + 1][0], pars[layer + 1, 0], *operands,
            )
            term_list[2 * layer + 2] = terms[:4] / head_count
        half = half_sum(keep, send)
        by_chunk = aligned and layer == 0
        more = (dp_count // 2, 3, rows, width)
        outs = [more] * 2 + [chunk] * 2 if by_chunk else [whole_grads]
        above = tuple(attn_grads[layer + 1]) if by_chunk else ()
        zero, *ffn_grads = call(
            lambda *refs, count=len(above): feed_grads_kernel(count, *refs),
            (shape(1, 1, dtype=F32),) + tuple(shape(*dims) for dims in outs), "feed_grads",
            grid=(steps,),
            in_specs=[smem(), whole(*flat), whole(*flat), act_spec, act_spec, whole(row_len, 1)]
            + [pl.BlockSpec(memory_space=pl.ANY)] * 2
            + [whole(*array.shape) for array in above],
            out_specs=[smem()] + [whole(*dims) for dims in outs],
            scratch_shapes=[
                pltpu.VMEM((width, row_len), BF),
                pltpu.VMEM(whole_grads if by_chunk else (8, 128), BF),
            ],
        )(dp_index, grad_b, second, active, g_up, row_routes, half, attn_all, *above)
        mine, other = other_half(half, zero)
        if by_chunk:
            up_send, up_keep, down_send, down_keep = ffn_grads
            up_list = [(up_keep, swap(up_send, "dp", 1))]
            down_list = [(down_keep, swap(down_send, "dp", 2))]
        else:
            ffn_shards[layer] = lax.psum_scatter(
                tie(ffn_grads[0], mine), "dp", scatter_dimension=1, tiled=True
            )
        gradient, terms, m_b, g_qkv, keep, send = call(
            lambda *refs, layer=layer: attend_back_kernel(layer, *refs),
            fresh_terms + (shape(*flat), shape(row_len, KEPT)) + both_halves,
            "attend_back",
            grid=(1,),
            in_specs=[smem(), whole(*flat)] + half_specs
            + [whole(*flat), whole(4, width), whole(row_len, 1)]
            + [whole(row_len, KEPT), whole(8, row_len), attn_spec(layer), out_spec] + seg_specs,
            out_specs=[whole(*flat), whole(8, width), whole(*flat), whole(row_len, KEPT)]
            + half_specs,
            scratch_shapes=[total, pltpu.VMEM((KEPT, row_len), BF), wide],
        )(
            head, gradient, mine, other, middle, pars[layer, 1], row_routes,
            qkv, lse, gathered[0], out_w, seg_col, seg_row,
        )
        term_list[2 * layer + 1] = terms[:4] / head_count
        markers["attend", layer] = keep
        if layer:
            half = half_sum(keep, send)
        else:
            half = keep + swap(send, "head", 1).astype(F32)
        outs = [narrow] * 2 if aligned else [(width, width)]
        zero, *qkv_grads = call(
            attend_grads_kernel,
            (shape(1, 1, dtype=F32),) + tuple(shape(*dims) for dims in outs),
            "attend_grads",
            grid=(1,),
            in_specs=[
                smem(), smem(), whole(*flat), whole(row_len, KEPT),
                pl.BlockSpec((1, width, row_len), lambda i, layer=layer: (layer, 0, 0)),
                whole(*flat), pl.BlockSpec(memory_space=pl.ANY),
            ],
            out_specs=[smem()] + [whole(*dims) for dims in outs],
            scratch_shapes=[pltpu.VMEM((width, width), BF)],
        )(head, dp_index, first, g_qkv, attn_all, m_b, half)
        if layer:
            mine, other = other_half(half, zero)
        attn_grads[layer] = qkv_grads
    first_out = ()
    if aligned:
        first_out = (attn_grads[0][0], output)
    own, recv = own_sum(half, head_at)
    grad_input, terms = call(
        last_norm_kernel,
        (shape(tok_count, width, dtype=F32), shape(8, width, dtype=F32)),
        "last_norm",
        in_specs=[smem()] + [vmem] * 6 + [pl.BlockSpec(memory_space=pl.ANY)] * len(first_out),
    )(head, gradient, own, recv, tokens, pars[0, 0], routes, *first_out)
    term_list[0] = terms[:4]
    if aligned:
        up_list = add_split(dp_index, up_list, 1, (grad_input,))
        down_list = add_split(dp_index, down_list, 0, (up_list[0][0],))

    terms = jnp.concatenate(term_list, axis=0)
    if not aligned:
        terms = terms.reshape(8 * layers, dp_count, rows)
        terms = lax.all_to_all(jnp.transpose(terms, (1, 0, 2)), "dp", 0, 0, tiled=True)
        terms = lax.psum(jnp.sum(terms, axis=0), "head").reshape(layers, 2, 2, 2, rows)
        grad_gain, grad_bias = terms[:, :, 0], terms[:, :, 1]

    if aligned:
        dims = (
            (layers, rows, 3 * width), (layers, rows, width),
            (layers, 2, rows, hidden_all), (layers, 2, down_rows, width),
        )

        def slot(dims, layer):
            return pl.BlockSpec((1,) + dims[1:], lambda i: (layer,) + (0,) * (len(dims) - 1))

        def unpack(kernel, pieces, old, outs, specs, name, scratch=()):
            return call(
                kernel, [shape(*out, dtype=F32) for out in outs], name,
                grid=(1,),
                in_specs=[smem()] + [whole(*piece.shape) for piece in pieces]
                + [pl.BlockSpec(memory_space=pl.ANY)] * len(old),
                out_specs=specs,
                scratch_shapes=[pltpu.VMEM((4,) + array, BF) for array in scratch],
                input_output_aliases={1 + len(pieces) + at: at for at in range(len(old))},
            )(head, *pieces, *old)

        ffn1 = tie(ffn_shards[1], down_list[0][0])
        up_list = add_split(dp_index, up_list, 2, (ffn1,))
        down_list = add_split(dp_index, down_list, 2, (up_list[0][0],))
        term_lanes = jnp.pad(terms.T.astype(BF), ((0, 0), (0, 128 - terms.shape[0])))
        term_send, term_keep = by_pairs(term_lanes, dp_at, dp_count)
        qkv_send, qkv_keep = attn_grads[0]
        last = [(term_keep, swap(term_send, "dp", 1)), (qkv_keep, swap(qkv_send, "dp", 1))]
        last = add_split(dp_index, last, 1, (down_list[0][0],))
        ffn1 = lax.all_gather(ffn1, "head", axis=0)
        grad_up, grad_down = unpack(
            unpack_later_kernel, [ffn1], (),
            (dims[2], dims[3]), [slot(dims[2], 1), slot(dims[3], 1)], "unpack_later",
        )
        last = add_split(dp_index, last, 2, (grad_up,))
        up0, down0 = add_each([up_list[0], down_list[0]], (last[0][0],))
        down0 = lax.all_gather(down0, "head", axis=0)
        up0 = head_pieces(up0)
        last = head_pieces(add_last(last))
        grad_up, grad_qkv, grad_out = unpack(
            unpack_up_kernel, up0, (grad_up,),
            (dims[2], dims[0], dims[1]), [slot(dims[2], 0), slot(dims[0], 1), slot(dims[1], 1)],
            "unpack_up", [up0[0].shape],
        )
        (grad_down,) = unpack(
            unpack_down_kernel, [down0], (grad_down,), (dims[3],), [slot(dims[3], 0)],
            "unpack_down",
        )
        grad_qkv, grad_out, grad_gain, grad_bias = unpack(
            unpack_attn_kernel, last, (grad_qkv, grad_out),
            (dims[0], dims[1], (layers, 2, 2, rows), (layers, 2, 2, rows)),
            [slot(dims[0], 0), slot(dims[1], 0)] + [whole(layers, 2, 2, rows)] * 2,
            "unpack_attn", [last[0].shape],
        )
        weight_grads = (grad_qkv, grad_out, grad_up, grad_down)
    else:
        grad_qkv, grad_out, grad_up, grad_down = [], [], [], []
        for layer in range(layers):
            attn_shard = lax.psum_scatter(
                attn_grads[layer][0], "dp", scatter_dimension=0, tiled=True
            )
            ffn_all = lax.all_gather(ffn_shards[layer], "head", axis=0)
            attn_all = lax.all_gather(attn_shard, "head", axis=0)
            taken = attn_all[:, :, : 3 * head_cols].reshape(head_count, rows, 3, head_cols)
            grad_qkv.append(jnp.transpose(taken, (1, 2, 0, 3)).reshape(rows, 3 * width))
            taken = jnp.transpose(attn_all[:, :, 3 * head_cols :], (1, 0, 2))
            grad_out.append(taken.reshape(rows, width))
            taken = ffn_all[:, :2].reshape(head_count, 2, rows, dp_count, sub)
            taken = jnp.transpose(taken, (1, 2, 3, 0, 4))
            grad_up.append(taken.reshape(2, rows, hidden_all))
            taken = jnp.transpose(ffn_all[:, 2:], (1, 0, 2, 3))
            grad_down.append(taken.reshape(2, down_rows, width))
        weight_grads = tuple(
            jnp.stack(part).astype(F32) for part in (grad_qkv, grad_out, grad_up, grad_down)
        )
    return (output, grad_input, grad_gain, grad_bias) + weight_grads


def solution(mesh):
    tokens = P(("dp", "head"), None)
    by_dp = (
        P(None, None, None, "dp"),
        P(None, None, None, "dp"),
        P(None, "dp", None),
        P(None, "dp", None),
        P(None, None, "dp", None),
        P(None, None, "dp", None),
    )
    return jax.shard_map(
        body,
        mesh=mesh,
        in_specs=(tokens, P("dp", None), tokens) + by_dp + (tokens,),
        out_specs=(tokens, tokens) + by_dp,
        check_vma=False,
    )
```

```python
import jax
import jax.numpy as jnp
from jax import lax
from jax.experimental import pallas as pl
from jax.experimental.pallas import tpu as pltpu
from jax.sharding import PartitionSpec as P

H = 12
HD = 64
BF = jnp.bfloat16
F32 = jnp.float32
VMEM_BYTES = 50 * 1024 * 1024
COLS = 256
PACKED = 768
KEPT = 640

far_below = -1e30
scale = HD**-0.5


def nn(a, b):
    return lax.dot_general(a, b, (((1,), (0,)), ((), ())), preferred_element_type=F32)


def nt(a, b):
    return lax.dot_general(a, b, (((1,), (1,)), ((), ())), preferred_element_type=F32)


def tn(a, b):
    return lax.dot_general(a, b, (((0,), (0,)), ((), ())), preferred_element_type=F32)


def shape(*dims, dtype=BF):
    return jax.ShapeDtypeStruct(dims, dtype)


def smem():
    return pl.BlockSpec(memory_space=pltpu.SMEM)


def whole(*dims):
    return pl.BlockSpec(dims, lambda i: (0,) * len(dims))


def call(kernel, out_shape, name, micros=0, **rest):
    return pl.pallas_call(
        kernel,
        out_shape=out_shape,
        name=name,
        compiler_params=pltpu.CompilerParams(vmem_limit_bytes=VMEM_BYTES),
        cost_estimate=pl.CostEstimate(
            flops=micros * 1_000_000_000, bytes_accessed=0, transcendentals=0
        ),
        **rest,
    )


def unit_of(values):
    centred = values - jnp.mean(values, axis=-1, keepdims=True)
    inv_std = lax.rsqrt(jnp.mean(centred * centred, axis=-1, keepdims=True) + 1e-05)
    return centred * inv_std, inv_std


def norm_rows(values, par_ref, second):
    gain = jnp.where(second, par_ref[1:2, :], par_ref[0:1, :])
    bias = jnp.where(second, par_ref[3:4, :], par_ref[2:3, :])
    return (unit_of(values)[0] * gain + bias).astype(BF)


def norm_back_rows(grad, incoming, base, par_ref, second, terms_ref):
    unit, inv_std = unit_of(base)
    scaled = incoming * jnp.where(second, par_ref[1:2, :], par_ref[0:1, :])
    fresh = grad + inv_std * (
        scaled
        - jnp.mean(scaled, axis=-1, keepdims=True)
        - unit * jnp.mean(scaled * unit, axis=-1, keepdims=True)
    )
    gain_term = incoming * unit
    zero = jnp.zeros_like(incoming)
    terms_ref[0:1, :] += jnp.sum(jnp.where(second, zero, gain_term), axis=0, keepdims=True)
    terms_ref[1:2, :] += jnp.sum(jnp.where(second, gain_term, zero), axis=0, keepdims=True)
    terms_ref[2:3, :] += jnp.sum(jnp.where(second, zero, incoming), axis=0, keepdims=True)
    terms_ref[3:4, :] += jnp.sum(jnp.where(second, incoming, zero), axis=0, keepdims=True)
    return fresh


def each_block(head, mine_ref, other_ref, act):
    core = head & 1
    pairs, rows = mine_ref.shape[0], mine_ref.shape[1]
    for pair in range(pairs):
        for ref, side in ((mine_ref, core), (other_ref, 1 - core)):
            at = pl.multiple_of((2 * pair + side) * rows, rows)
            act(pl.ds(at, rows), ref[pair].astype(F32))


def split_out(head, total_ref, keep_ref, send_ref):
    core = head & 1
    pairs, rows = keep_ref.shape[0], keep_ref.shape[1]
    for pair in range(pairs):
        at = pl.multiple_of((2 * pair + core) * rows, rows)
        keep_ref[pair] = total_ref[pl.ds(at, rows), :]
        at = pl.multiple_of((2 * pair + 1 - core) * rows, rows)
        send_ref[pair] = total_ref[pl.ds(at, rows), :].astype(BF)


def attend_math(first_ref, w_ref, segc_ref, segr_ref, qkv_ref, attn_ref, lse_ref):
    heads = attn_ref.shape[0] // HD
    qkv = nn(first_ref[...], w_ref[:, : qkv_ref.shape[1]]).astype(BF)
    qkv_ref[...] = qkv
    turned = qkv.T
    same = segc_ref[...] == segr_ref[...]
    for j in range(heads):
        at_q, at_k, at_v = (HD * (j + heads * part) for part in range(3))
        scores = nn(qkv[:, at_k : at_k + HD], turned[at_q : at_q + HD]) * scale
        scores = jnp.where(same, scores, far_below)
        top = jnp.max(scores, axis=0, keepdims=True)
        exponent = jnp.exp(scores - top)
        total = jnp.sum(exponent, axis=0, keepdims=True)
        prob = (exponent / total).astype(BF)
        attn_ref[HD * j : HD * (j + 1), :] = nn(turned[at_v : at_v + HD], prob).astype(BF)
        lse_ref[j : j + 1, :] = top + jnp.log(total)


def join_lanes(blocks_ref, layer, out_ref):
    cols = out_ref.shape[1] // blocks_ref.shape[0]
    for part in range(blocks_ref.shape[0]):
        out_ref[:, part * cols : (part + 1) * cols] = blocks_ref[
            part, :, layer * cols : (layer + 1) * cols
        ]


def attend_first_kernel(
    tok_ref, small_ref, route_ref, w_ref, segc_ref, segr_ref,
    par_ref, first_ref, qkv_ref, attn_ref, lse_ref,
):
    turned = small_ref[...].astype(F32).T
    par_ref[...] = turned[: par_ref.shape[0]]
    first_ref[...] = norm_rows(tok_ref[...].astype(F32), par_ref, route_ref[...] == 1)
    attend_math(first_ref, w_ref, segc_ref, segr_ref, qkv_ref, attn_ref, lse_ref)


def project_kernel(head_ref, attn_ref, wo_ref, keep_ref, send_ref, total_ref, wide_ref):
    join_lanes(wo_ref, 0, wide_ref)
    total_ref[...] = tn(attn_ref[...], wide_ref[...])
    split_out(head_ref[0], total_ref, keep_ref, send_ref)


def attend_kernel(
    layer, head_ref, base_ref, mine_ref, other_ref, par_ref, route_ref, w_ref, wo_ref, segc_ref, segr_ref,
    stream_ref, first_ref, qkv_ref, attn_ref, lse_ref, keep_ref, send_ref, total_ref, wide_ref,
):
    def act(rows, fresh):
        values = base_ref[rows, :].astype(F32) + fresh
        stream_ref[rows, :] = values
        first_ref[rows, :] = norm_rows(values, par_ref, route_ref[rows, :] == 1)

    each_block(head_ref[0], mine_ref, other_ref, act)
    attend_math(first_ref, w_ref, segc_ref, segr_ref, qkv_ref, attn_ref, lse_ref)
    join_lanes(wo_ref, layer, wide_ref)
    total_ref[...] = tn(attn_ref[...], wide_ref[...])
    split_out(head_ref[0], total_ref, keep_ref, send_ref)


def split_sides(dp_ref, bit, grads_ref, send_ref, keep_ref):
    side = (dp_ref[0] >> bit) & 1
    rows = send_ref.shape[-2]
    for out_ref, flip in ((send_ref, 1), (keep_ref, 0)):
        for place in range(out_ref.shape[0]):
            low = place % (1 << bit)
            block = ((place - low) << 1) + low + ((side ^ flip) << bit)
            at = pl.ds(pl.multiple_of(block * rows, 16), rows)
            if len(out_ref.shape) == 3:
                out_ref[place] = grads_ref[at, :]
            else:
                for member in range(out_ref.shape[1]):
                    out_ref[place, member] = grads_ref[member, at, :]


def attend_back_kernel(
    layer, head_ref, grad_ref, mine_ref, other_ref, base_ref, par_ref, route_ref,
    qkv_ref, lse_ref, w_ref, wo_ref, segc_ref, segr_ref,
    fresh_ref, terms_ref, m_ref, gqkv_ref, keep_ref, send_ref, total_ref, turned_ref, wide_ref,
):
    terms_ref[...] = jnp.zeros_like(terms_ref)

    def act(rows, incoming):
        fresh = norm_back_rows(
            grad_ref[rows, :].astype(F32), incoming, base_ref[rows, :].astype(F32),
            par_ref, route_ref[rows, :] == 1, terms_ref,
        )
        fresh_ref[rows, :] = fresh
        m_ref[rows, :] = fresh.astype(BF)

    each_block(head_ref[0], mine_ref, other_ref, act)
    join_lanes(wo_ref, layer, wide_ref)
    heads = wide_ref.shape[0] // HD
    grad_attn = nt(wide_ref[...], m_ref[...]).astype(BF)
    qkv = qkv_ref[...]
    turned = qkv.T
    same = segc_ref[...] == segr_ref[...]
    for j in range(heads):
        at_q, at_k, at_v = (HD * (j + heads * part) for part in range(3))
        scores = nn(qkv[:, at_k : at_k + HD], turned[at_q : at_q + HD]) * scale
        prob = jnp.exp(jnp.where(same, scores, far_below) - lse_ref[j : j + 1, :])
        g_out = grad_attn[HD * j : HD * (j + 1)]
        g_prob = nn(qkv[:, at_v : at_v + HD], g_out)
        inner = jnp.sum(prob * g_prob, axis=0, keepdims=True)
        g_scores = (prob * (g_prob - inner)).astype(BF)
        g_q = nn(turned[at_k : at_k + HD], g_scores) * scale
        g_k = nt(turned[at_q : at_q + HD], g_scores) * scale
        g_v = nt(g_out, prob.astype(BF))
        turned_ref[at_q : at_q + HD, :] = g_q.astype(BF)
        turned_ref[at_k : at_k + HD, :] = g_k.astype(BF)
        turned_ref[at_v : at_v + HD, :] = g_v.astype(BF)
    used = 3 * heads * HD
    turned_ref[used:, :] = jnp.zeros((turned_ref.shape[0] - used, turned_ref.shape[1]), BF)
    g_qkv = turned_ref[...].T
    gqkv_ref[...] = g_qkv
    total_ref[...] = nt(g_qkv, w_ref[:, : g_qkv.shape[1]])
    split_out(head_ref[0], total_ref, keep_ref, send_ref)


def attend_grads_kernel(
    head_ref, dp_ref, first_ref, gqkv_ref, attn_ref, m_ref, after_ref, *rest
):
    zero_ref, *gw_refs, grads_ref = rest
    zero_ref[0, 0] = 0.0
    into_ref = gw_refs[0] if len(gw_refs) == 1 else grads_ref
    cols = into_ref.shape[1] // 4
    grads = tn(first_ref[...], gqkv_ref[...]).astype(BF)
    into_ref[:, : 3 * cols] = grads[:, : 3 * cols]
    for j in range(4):

        @pl.when(head_ref[0] == j)
        def _():
            into_ref[:, 3 * cols :] = nn(
                attn_ref[0], m_ref[:, j * cols : (j + 1) * cols]
            ).astype(BF)

    if len(gw_refs) > 1:
        split_sides(dp_ref, 0, grads_ref, *gw_refs)


def add_up(term, total_ref):
    step = pl.program_id(0)

    @pl.when(step == 0)
    def _():
        total_ref[...] = term

    @pl.when(step > 0)
    def _():
        total_ref[...] += term


def feed_kernel(
    head_ref, base_ref, mine_ref, other_ref, par_ref, route_ref, wu0_ref, wu1_ref, wd0_ref, wd1_ref,
    middle_ref, x_ref, act_ref, slope_ref, keep_ref, send_ref, total_ref,
):
    step = pl.program_id(0)

    @pl.when(step == 0)
    def _():
        def act(rows, fresh):
            values = base_ref[rows, :].astype(F32) + fresh
            middle_ref[rows, :] = values
            x_ref[rows, :] = norm_rows(values, par_ref, route_ref[rows, :] == 1)

        each_block(head_ref[0], mine_ref, other_ref, act)

    second = route_ref[...] == 1
    x = x_ref[...]
    up = jnp.where(second, nn(x, wu1_ref[...]), nn(x, wu0_ref[...]))
    phi = 0.5 * (1.0 + lax.erf(up * 0.7071067811865476))
    active = (up * phi).astype(BF)
    act_ref[...] = active
    slope_ref[...] = (phi + up * jnp.exp(-0.5 * up * up) * 0.3989422804014327).astype(BF)
    zero = jnp.zeros_like(active)
    term = nn(jnp.where(second, zero, active), wd0_ref[...])
    term += nn(jnp.where(second, active, zero), wd1_ref[...])
    add_up(term, total_ref)

    @pl.when(step == pl.num_programs(0) - 1)
    def _():
        split_out(head_ref[0], total_ref, keep_ref, send_ref)


def feed_back_math(
    head_ref, g_ref, slope_ref, wu0_ref, wu1_ref, wd0_ref, wd1_ref, route_ref,
    gup_ref, keep_ref, send_ref, total_ref,
):
    second = route_ref[...] == 1
    g_b = g_ref[...]
    g_up = jnp.where(second, nt(g_b, wd1_ref[...]), nt(g_b, wd0_ref[...]))
    g_up = (g_up * slope_ref[...].astype(F32)).astype(BF)
    gup_ref[...] = g_up
    zero = jnp.zeros_like(g_up)
    term = nt(jnp.where(second, zero, g_up), wu0_ref[...])
    term += nt(jnp.where(second, g_up, zero), wu1_ref[...])
    add_up(term, total_ref)

    @pl.when(pl.program_id(0) == pl.num_programs(0) - 1)
    def _():
        split_out(head_ref[0], total_ref, keep_ref, send_ref)


def feed_back_first_kernel(
    head_ref, g_ref, slope_ref, wu0_ref, wu1_ref, wd0_ref, wd1_ref, route_ref,
    gup_ref, keep_ref, send_ref, total_ref,
):
    feed_back_math(
        head_ref, g_ref, slope_ref, wu0_ref, wu1_ref, wd0_ref, wd1_ref, route_ref,
        gup_ref, keep_ref, send_ref, total_ref,
    )


def feed_back_kernel(
    head_ref, grad_ref, mine_ref, other_ref, base_ref, par_ref,
    slope_ref, wu0_ref, wu1_ref, wd0_ref, wd1_ref, route_ref,
    fresh_ref, terms_ref, g_ref, gup_ref, keep_ref, send_ref, total_ref,
):
    @pl.when(pl.program_id(0) == 0)
    def _():
        terms_ref[...] = jnp.zeros_like(terms_ref)

        def act(rows, incoming):
            fresh = norm_back_rows(
                grad_ref[rows, :], incoming, base_ref[rows, :],
                par_ref, route_ref[rows, :] == 1, terms_ref,
            )
            fresh_ref[rows, :] = fresh
            g_ref[rows, :] = fresh.astype(BF)

        each_block(head_ref[0], mine_ref, other_ref, act)

    feed_back_math(
        head_ref, g_ref, slope_ref, wu0_ref, wu1_ref, wd0_ref, wd1_ref, route_ref,
        gup_ref, keep_ref, send_ref, total_ref,
    )


def feed_grads_kernel(
    carried, dp_ref, g_ref, x_ref, act_ref, gup_ref, route_ref, after_ref, attn_ref, *rest
):
    above, (zero_ref, *outs, turned_ref, grads_ref) = rest[:carried], rest[carried:]
    zero_ref[0, 0] = 0.0
    step = pl.program_id(0)
    cols = act_ref.shape[1]
    second = route_ref[...] == 1

    @pl.when(step == 0)
    def _():
        turned_ref[...] = x_ref[...].T

    into_ref = outs[0] if len(outs) == 1 else grads_ref
    active = act_ref[...]
    g_up = gup_ref[...]
    zero = jnp.zeros_like(g_up)
    here = pl.ds(pl.multiple_of(step * cols, cols), cols)
    for expert in range(2):
        mine = second if expert else jnp.logical_not(second)
        into_ref[expert, :, here] = nn(turned_ref[...], jnp.where(mine, g_up, zero)).astype(BF)
        into_ref[2 + expert, here, :] = tn(jnp.where(mine, active, zero), g_ref[...]).astype(BF)

    @pl.when(step == pl.num_programs(0) - 1)
    def _():
        if len(outs) > 1:
            split_sides(dp_ref, 0, grads_ref.at[:2], outs[0].at[:, :2], outs[1].at[:, :2])
            for from_ref, to_ref in zip(above, outs):
                to_ref[:, 2] = from_ref[...]
            split_sides(dp_ref, 1, grads_ref.at[2:], outs[2], outs[3])


def last_add_kernel(head_ref, middle_ref, own_ref, recv_ref, out_ref):
    rows = out_ref.shape[0]
    at = pl.multiple_of(head_ref[0] * rows, rows)
    out_ref[...] = middle_ref[pl.ds(at, rows), :] + own_ref[...] + recv_ref[...].astype(F32)


def last_norm_kernel(head_ref, grad_ref, own_ref, recv_ref, tok_ref, par_ref, route_ref, *refs):
    out_ref, terms_ref = refs[-2:]
    terms_ref[...] = jnp.zeros_like(terms_ref)
    rows = out_ref.shape[0]
    at = pl.multiple_of(head_ref[0] * rows, rows)
    out_ref[...] = norm_back_rows(
        grad_ref[pl.ds(at, rows), :], own_ref[...] + recv_ref[...].astype(F32),
        tok_ref[...].astype(F32), par_ref, route_ref[...] == 1, terms_ref,
    )


def add_split_kernel(count, bit, dp_ref, *refs):
    inputs, (send_ref, keep_ref) = refs[:count], refs[-2:]
    side = (dp_ref[0] >> bit) & 1
    for out_ref, flip in ((send_ref, 1), (keep_ref, 0)):
        for place in range(out_ref.shape[0]):
            at = 2 * place + (side ^ flip)
            lane = 0
            for one_ref, two_ref in zip(inputs[::2], inputs[1::2]):
                cols = one_ref.shape[-1]
                total = (one_ref[at].astype(F32) + two_ref[at].astype(F32)).astype(BF)
                out_ref[place, ..., lane : lane + cols] = total
                lane += cols


def add_last_kernel(count, *refs):
    inputs, out_ref = refs[:count], refs[-1]
    lane = 0
    for one_ref, two_ref in zip(inputs[::2], inputs[1::2]):
        cols = one_ref.shape[-1]
        total = (one_ref[0].astype(F32) + two_ref[0].astype(F32)).astype(BF)
        out_ref[..., lane : lane + cols] = total
        lane += cols


def add_each_kernel(count, *refs):
    for group in range(count):
        one_ref, two_ref = refs[2 * group : 2 * group + 2]
        total = one_ref[0].astype(F32) + two_ref[0].astype(F32)
        refs[group - count][...] = total.astype(BF)


def tie_kernel(array_ref, after_ref, out_ref):
    pass


def pack_kernel(head_ref, up_ref, down_ref, *refs):
    out_ref, tall_ref = refs[-2:]
    width = down_ref.shape[3]
    count = 4
    hidden = up_ref.shape[3] // count
    sub = down_ref.shape[2] // count
    for j in range(count):

        @pl.when(head_ref[0] == j)
        def _():
            for expert in range(2):
                to = (2 + expert) * hidden
                out_ref[:, to : to + width] = down_ref[0, expert, j * sub : (j + 1) * sub, :]
                for block in range(hidden // sub):
                    at = block * sub * count + j * sub
                    to = expert * hidden + block * sub
                    out_ref[:, to : to + sub] = up_ref[0, expert, :, at : at + sub]
            if out_ref.shape[1] > 4 * hidden:
                qkv_ref, wo_ref, small_ref = refs[:3]
                cols = width // count
                for layer in range(qkv_ref.shape[0]):
                    to = 4 * hidden + layer * PACKED
                    for part in range(3):
                        at = part * width + j * cols
                        out_ref[:, to : to + cols] = qkv_ref[layer, :, at : at + cols]
                        to += cols
                    out_ref[:, to : to + cols] = wo_ref[layer, :, j * cols : (j + 1) * cols]
                tall_ref[...] = jnp.zeros_like(tall_ref)
                tall_ref[: small_ref.shape[0], : small_ref.shape[1]] = small_ref[...].astype(F32)
                out_ref[:, 4 * hidden + qkv_ref.shape[0] * PACKED :] = tall_ref[...].T[
                    : out_ref.shape[0]
                ].astype(BF)


def gather_refs(head_ref, arrays, blocks_ref):
    for s in range(4):
        blocks_ref[head_ref[0] ^ s] = arrays[s][...]


def unpack_up(blocks_ref, gu_ref):
    sub = blocks_ref.shape[2]
    for h in range(4):
        for expert in range(2):
            for block in range(gu_ref.shape[3] // (4 * sub)):
                at = block * 4 * sub + h * sub
                gu_ref[0, expert, :, at : at + sub] = blocks_ref[
                    h, expert, :, block * sub : (block + 1) * sub
                ].astype(F32)


def unpack_down(blocks_ref, first, gd_ref):
    sub = blocks_ref.shape[2]
    for h in range(4):
        for expert in range(2):
            gd_ref[0, expert, h * sub : (h + 1) * sub, :] = blocks_ref[h, first + expert].astype(F32)


def unpack_qkv(block_of, gq_ref, go_ref):
    cols = go_ref.shape[2] // 4
    for h in range(4):
        for part in range(3):
            to = part * 4 * cols + h * cols
            gq_ref[0, :, to : to + cols] = block_of(h, part * cols, cols).astype(F32)
        go_ref[0, :, h * cols : (h + 1) * cols] = block_of(h, 3 * cols, cols).astype(F32)


def unpack_later_kernel(head_ref, ffn_ref, gu_ref, gd_ref):
    unpack_up(ffn_ref, gu_ref)
    unpack_down(ffn_ref, 2, gd_ref)


def unpack_up_kernel(head_ref, *refs):
    gu_ref, gq_ref, go_ref, blocks_ref = refs[-4:]
    gather_refs(head_ref, refs[:4], blocks_ref)
    unpack_up(blocks_ref, gu_ref)
    unpack_qkv(lambda h, at, cols: blocks_ref[h, 2, :, at : at + cols], gq_ref, go_ref)


def unpack_down_kernel(head_ref, blocks_ref, *refs):
    unpack_down(blocks_ref, 0, refs[-1])


def unpack_attn_kernel(head_ref, *refs):
    gq_ref, go_ref, gain_ref, bias_ref, blocks_ref = refs[-5:]
    gather_refs(head_ref, refs[:4], blocks_ref)
    unpack_qkv(lambda h, at, cols: blocks_ref[h, :, 128 + at : 128 + at + cols], gq_ref, go_ref)
    terms = blocks_ref[0, :, :128].astype(F32)
    for h in range(1, 4):
        terms += blocks_ref[h, :, :128].astype(F32)
    turned = terms.T
    for layer in range(2):
        for place in range(2):
            at = 8 * layer + 4 * place
            gain_ref[layer, place] = turned[at : at + 2]
            bias_ref[layer, place] = turned[at + 2 : at + 4]


def swap(array, axis, bits):
    count = lax.axis_size(axis)
    return lax.ppermute(array, axis, [(i, i ^ bits) for i in range(count)])


def half_sum(keep, send):
    return (keep + swap(send, "head", 1).astype(F32)).astype(BF)


def other_half(half, zero=None):
    recv = swap(half, "head", 2).astype(F32)
    if zero is not None:
        recv = recv + zero.reshape(())
    mine = (half.astype(F32) + recv).astype(BF)
    return mine, swap(mine, "head", 1)


def head_sum(keep, send):
    return other_half(half_sum(keep, send))


def own_sum(half, head_at):
    pair = head_at // 2
    recv = swap(lax.dynamic_index_in_dim(half, 1 - pair, 0, keepdims=False).astype(BF), "head", 2)
    return lax.dynamic_index_in_dim(half, pair, 0, keepdims=False), recv


def spread(array, axis):
    copies = jnp.broadcast_to(array[None], (lax.axis_size(axis),) + array.shape)
    return lax.all_to_all(copies, axis, 0, 0, tiled=True)


def head_pieces(shard):
    across = swap(shard, "head", 2)
    return [shard, swap(shard, "head", 1), across, swap(across, "head", 1)]


def by_pairs(grads, dp_at, dp_count):
    sides = grads.reshape(dp_count // 2, 2, -1, grads.shape[-1])
    side = dp_at % 2
    return (
        lax.dynamic_index_in_dim(sides, 1 - side, 1, keepdims=False),
        lax.dynamic_index_in_dim(sides, side, 1, keepdims=False),
    )


def add_split(dp_index, lists, bit, after):
    flat = [array for pair in lists for array in pair]
    lanes = sum(keep.shape[-1] for keep, _ in lists)
    dims = (flat[0].shape[0] // 2,) + flat[0].shape[1:-1] + (lanes,)
    vmem = pl.BlockSpec(memory_space=pltpu.VMEM)
    send, keep = call(
        lambda *refs: add_split_kernel(len(flat), bit, *refs), (shape(*dims),) * 2, "add_split",
        in_specs=[smem()] + [vmem] * len(flat) + [pl.BlockSpec(memory_space=pl.ANY)] * len(after),
    )(dp_index, *flat, *after)
    return [(keep, swap(send, "dp", 1 << bit))]


def add_last(lists, after=()):
    flat = [array for pair in lists for array in pair]
    lanes = sum(keep.shape[-1] for keep, _ in lists)
    vmem = pl.BlockSpec(memory_space=pltpu.VMEM)
    return call(
        lambda *refs: add_last_kernel(len(flat), *refs),
        shape(*flat[0].shape[1:-1], lanes), "add_last",
        in_specs=[vmem] * len(flat) + [pl.BlockSpec(memory_space=pl.ANY)] * len(after),
    )(*flat, *after)


def add_each(groups, after):
    flat = [array for pair in groups for array in pair]
    vmem = pl.BlockSpec(memory_space=pltpu.VMEM)
    return call(
        lambda *refs: add_each_kernel(len(groups), *refs),
        [shape(*keep.shape[1:]) for keep, _ in groups], "add_each",
        in_specs=[vmem] * len(flat) + [pl.BlockSpec(memory_space=pl.ANY)] * len(after),
    )(*flat, *after)


def tie(array, after):
    return call(
        tie_kernel, shape(*array.shape), "tie",
        in_specs=[pl.BlockSpec(memory_space=pl.ANY)] * 2,
        out_specs=pl.BlockSpec(memory_space=pl.ANY),
        input_output_aliases={0: 0},
    )(array, after)


def body(tokens, segments, routes, norm_gain, norm_bias, w_qkv, w_out, w_up, w_down, cotangent):
    dp_count = lax.axis_size("dp")
    head_count = lax.axis_size("head")
    head_at = lax.axis_index("head")
    dp_at = lax.axis_index("dp")
    head = head_at.reshape(1)
    dp_index = dp_at.reshape(1)
    tok_count, width = tokens.shape
    row_len = segments.shape[1]
    layers = norm_gain.shape[0]
    head_cols = H // head_count * HD
    hidden_all = w_up.shape[3]
    hidden = hidden_all // head_count
    rows = w_qkv.shape[1]
    down_rows = w_down.shape[2]
    sub = down_rows // head_count
    steps = hidden // COLS
    aligned = rows % 16 == 0 and dp_count == 8 and head_count == 4 and layers == 2

    small = jnp.stack([norm_gain, norm_bias], axis=2).reshape(layers * 8, rows)

    seg_col = segments.reshape(row_len, 1)
    seg_row = segments.reshape(1, row_len)
    route_lanes = jnp.pad(routes.astype(BF), ((0, 0), (0, 127)))
    both = spread(jnp.concatenate([tokens, cotangent, route_lanes], axis=1), "head")
    both = both.reshape(row_len, 2 * width + 128)
    row_tokens = both[:, :width]
    row_cotangent = both[:, width : 2 * width]
    row_routes = both[:, 2 * width : 2 * width + 1].astype(jnp.int32)

    packs = []
    for layer in range(layers):
        extra = (w_qkv, w_out, small) if layer == 0 else ()
        first = (row_tokens, row_cotangent, row_routes) if layer else ()
        lanes = 4 * width + (0 if layer else layers * PACKED + 128)
        if aligned:
            packs.append(
                call(
                    pack_kernel,
                    shape(rows, lanes),
                    "pack",
                    grid=(1,),
                    in_specs=[
                        smem(),
                        pl.BlockSpec(
                            (1, 2, rows, hidden_all), lambda i, layer=layer: (layer, 0, 0, 0)
                        ),
                        pl.BlockSpec(
                            (1, 2, down_rows, width), lambda i, layer=layer: (layer, 0, 0, 0)
                        ),
                    ]
                    + [whole(*array.shape) for array in extra]
                    + [pl.BlockSpec(memory_space=pl.ANY)] * len(first),
                    out_specs=whole(rows, lanes),
                    scratch_shapes=[pltpu.VMEM((128, 128), F32)],
                )(head, w_up, w_down, *extra, *first)
            )
        else:
            taken = lax.dynamic_index_in_dim(
                w_up[layer].reshape(2, rows, dp_count, head_count, sub), head_at, 3, keepdims=False
            ).reshape(2, rows, hidden)
            down = lax.dynamic_index_in_dim(
                w_down[layer].reshape(2, head_count, sub, width), head_at, 1, keepdims=False
            )
            parts = [taken[0], taken[1], down[0], down[1]]
            for at in range(layers if layer == 0 else 0):
                taken = lax.dynamic_index_in_dim(
                    w_qkv[at].reshape(rows, 3, head_count, head_cols), head_at, 2, keepdims=False
                )
                out = lax.dynamic_index_in_dim(
                    w_out[at].reshape(rows, head_count, head_cols), head_at, 1, keepdims=False
                )
                parts += [taken.reshape(rows, 3 * head_cols), out]
            if layer == 0:
                parts.append(jnp.pad(small.T, ((0, 0), (0, 128 - layers * 8))))
            packs.append(jnp.concatenate(parts, axis=1))
    gathered = [lax.all_gather(pack, "dp", axis=0, tiled=True) for pack in packs]
    taken = [
        gathered[0][:, at : at + head_cols]
        for at in (4 * width + layer * PACKED + 3 * head_cols for layer in range(layers))
    ]
    out_w = lax.all_to_all(
        jnp.concatenate(taken, axis=1).reshape(head_count, head_cols, layers * head_cols),
        "head", 0, 0, tiled=True,
    )

    pairs = head_count // 2
    flat = (row_len, width)
    halves = (pairs, tok_count, width)
    both_halves = (shape(*halves, dtype=F32), shape(*halves))
    half_specs = [whole(*halves), whole(*halves)]
    per_expert = width // COLS
    weight_specs = [
        pl.BlockSpec((width, COLS), lambda i: (0, i)),
        pl.BlockSpec((width, COLS), lambda i: (0, per_expert + i)),
        pl.BlockSpec((COLS, width), lambda i: (i, 2)),
        pl.BlockSpec((COLS, width), lambda i: (i, 3)),
    ]
    act_spec = pl.BlockSpec((row_len, COLS), lambda i: (0, i))
    total = pltpu.VMEM(flat, F32)
    vmem = pl.BlockSpec(memory_space=pltpu.VMEM)

    def attn_spec(layer):
        return pl.BlockSpec((width, PACKED), lambda i: (0, 4 * width // PACKED + layer))

    small_spec = pl.BlockSpec((width, 128), lambda i: (0, 4 * width // 128 + layers * PACKED // 128))
    out_spec = whole(head_count, head_cols, layers * head_cols)
    seg_specs = [whole(row_len, 1), whole(1, row_len)]
    wide = pltpu.VMEM((head_cols, width), BF)

    saved = []
    for layer in range(layers):
        kept = (
            shape(*flat), shape(row_len, KEPT), shape(head_cols, row_len),
            shape(8, row_len, dtype=F32),
        )
        kept_specs = [whole(*array.shape) for array in kept]
        if layer == 0:
            stream = row_tokens
            pars, first, qkv, attn, lse = call(
                attend_first_kernel, (shape(layers * 8, width, dtype=F32),) + kept, "attend_first",
                grid=(1,),
                in_specs=[whole(*flat), small_spec, whole(row_len, 1), attn_spec(0)] + seg_specs,
                out_specs=[whole(layers * 8, width)] + kept_specs,
            )(stream, gathered[0], row_routes, gathered[0], seg_col, seg_row)
            pars = pars.reshape(layers, 2, 4, width)
            keep, send = call(
                project_kernel, both_halves, "project",
                in_specs=[smem()] + [vmem] * 2,
                scratch_shapes=[total, wide],
            )(head, attn, out_w)
        else:
            stream, first, qkv, attn, lse, keep, send = call(
                lambda *refs, layer=layer: attend_kernel(layer, *refs),
                (shape(*flat, dtype=F32),) + kept + both_halves,
                "attend",
                grid=(1,),
                in_specs=[smem(), whole(*flat)] + half_specs
                + [whole(4, width), whole(row_len, 1), attn_spec(layer), out_spec] + seg_specs,
                out_specs=[whole(*flat)] + kept_specs + half_specs,
                scratch_shapes=[total, wide],
            )(
                head, middle, mine, other, pars[layer, 0], row_routes, gathered[0], out_w,
                seg_col, seg_row,
            )
        mine, other = head_sum(keep, send)
        middle, second, active, slope, keep, send = call(
            feed_kernel,
            (shape(*flat, dtype=F32), shape(*flat), shape(row_len, hidden), shape(row_len, hidden))
            + both_halves,
            "feed",
            grid=(steps,),
            in_specs=[smem(), whole(*flat)] + half_specs
            + [whole(4, width), whole(row_len, 1)] + weight_specs,
            out_specs=[whole(*flat), whole(*flat), act_spec, act_spec] + half_specs,
            scratch_shapes=[total],
        )(head, stream, mine, other, pars[layer, 1], row_routes, *[gathered[layer]] * 4)
        saved.append((stream, first, qkv, attn, lse, middle, second, active, slope))
        if layer + 1 < layers:
            mine, other = head_sum(keep, send)
    half = keep + swap(send, "head", 1).astype(F32)
    attn_all = lax.all_gather(
        jnp.stack([entry[3] for entry in saved]), "head", axis=1, tiled=True
    )
    own, recv = own_sum(half, head_at)
    output = call(
        last_add_kernel, shape(tok_count, width, dtype=F32), "last_add",
        in_specs=[smem()] + [vmem] * 3,
    )(head, middle, own, recv)

    term_list = [None] * (2 * layers)
    ffn_shards = [None] * layers
    attn_grads = [None] * layers
    markers = {}
    fresh_terms = (shape(*flat, dtype=F32), shape(8, width, dtype=F32))
    whole_grads = (4, width, hidden)
    chunk = (dp_count // 2, 2, rows, width)
    narrow = (dp_count // 2, rows, width)
    gradient = row_cotangent
    for layer in reversed(range(layers)):
        stream, first, qkv, attn, lse, middle, second, active, slope = saved[layer]
        operands = (slope,) + (gathered[layer],) * 4 + (row_routes,)
        operand_specs = [act_spec] + weight_specs + [whole(row_len, 1)]
        if layer == layers - 1:
            grad_b = gradient
            g_up, keep, send = call(
                feed_back_first_kernel, (shape(row_len, hidden),) + both_halves,
                "feed_back_first",
                grid=(steps,),
                in_specs=[smem(), whole(*flat)] + operand_specs,
                out_specs=[act_spec] + half_specs,
                scratch_shapes=[total],
            )(head, gradient, *operands)
        else:
            gradient, terms, grad_b, g_up, keep, send = call(
                feed_back_kernel,
                fresh_terms + (shape(*flat), shape(row_len, hidden)) + both_halves,
                "feed_back",
                grid=(steps,),
                in_specs=[smem(), whole(*flat)] + half_specs
                + [whole(*flat), whole(4, width)] + operand_specs,
                out_specs=[whole(*flat), whole(8, width), whole(*flat), act_spec] + half_specs,
                scratch_shapes=[total],
            )(
                head, gradient, mine, other, saved[layer + 1][0], pars[layer + 1, 0], *operands,
            )
            term_list[2 * layer + 2] = terms[:4] / head_count
        half = half_sum(keep, send)
        by_chunk = aligned and layer == 0
        more = (dp_count // 2, 3, rows, width)
        outs = [more] * 2 + [chunk] * 2 if by_chunk else [whole_grads]
        above = tuple(attn_grads[layer + 1]) if by_chunk else ()
        zero, *ffn_grads = call(
            lambda *refs, count=len(above): feed_grads_kernel(count, *refs),
            (shape(1, 1, dtype=F32),) + tuple(shape(*dims) for dims in outs), "feed_grads",
            grid=(steps,),
            in_specs=[smem(), whole(*flat), whole(*flat), act_spec, act_spec, whole(row_len, 1)]
            + [pl.BlockSpec(memory_space=pl.ANY)] * 2
            + [whole(*array.shape) for array in above],
            out_specs=[smem()] + [whole(*dims) for dims in outs],
            scratch_shapes=[
                pltpu.VMEM((width, row_len), BF),
                pltpu.VMEM(whole_grads if by_chunk else (8, 128), BF),
            ],
        )(dp_index, grad_b, second, active, g_up, row_routes, half, attn_all, *above)
        mine, other = other_half(half, zero)
        if by_chunk:
            up_send, up_keep, down_send, down_keep = ffn_grads
            up_list = [(up_keep, swap(up_send, "dp", 1))]
            down_list = [(down_keep, swap(down_send, "dp", 2))]
        else:
            ffn_shards[layer] = lax.psum_scatter(
                tie(ffn_grads[0], mine), "dp", scatter_dimension=1, tiled=True
            )
        gradient, terms, m_b, g_qkv, keep, send = call(
            lambda *refs, layer=layer: attend_back_kernel(layer, *refs),
            fresh_terms + (shape(*flat), shape(row_len, KEPT)) + both_halves,
            "attend_back",
            grid=(1,),
            in_specs=[smem(), whole(*flat)] + half_specs
            + [whole(*flat), whole(4, width), whole(row_len, 1)]
            + [whole(row_len, KEPT), whole(8, row_len), attn_spec(layer), out_spec] + seg_specs,
            out_specs=[whole(*flat), whole(8, width), whole(*flat), whole(row_len, KEPT)]
            + half_specs,
            scratch_shapes=[total, pltpu.VMEM((KEPT, row_len), BF), wide],
        )(
            head, gradient, mine, other, middle, pars[layer, 1], row_routes,
            qkv, lse, gathered[0], out_w, seg_col, seg_row,
        )
        term_list[2 * layer + 1] = terms[:4] / head_count
        markers["attend", layer] = keep
        if layer:
            half = half_sum(keep, send)
        else:
            half = keep + swap(send, "head", 1).astype(F32)
        outs = [narrow] * 2 if aligned else [(width, width)]
        zero, *qkv_grads = call(
            attend_grads_kernel,
            (shape(1, 1, dtype=F32),) + tuple(shape(*dims) for dims in outs),
            "attend_grads",
            grid=(1,),
            in_specs=[
                smem(), smem(), whole(*flat), whole(row_len, KEPT),
                pl.BlockSpec((1, width, row_len), lambda i, layer=layer: (layer, 0, 0)),
                whole(*flat), pl.BlockSpec(memory_space=pl.ANY),
            ],
            out_specs=[smem()] + [whole(*dims) for dims in outs],
            scratch_shapes=[pltpu.VMEM((width, width), BF)],
        )(head, dp_index, first, g_qkv, attn_all, m_b, half)
        if layer:
            mine, other = other_half(half, zero)
        attn_grads[layer] = qkv_grads
    first_out = ()
    if aligned:
        first_out = (attn_grads[0][0], output)
    own, recv = own_sum(half, head_at)
    grad_input, terms = call(
        last_norm_kernel,
        (shape(tok_count, width, dtype=F32), shape(8, width, dtype=F32)),
        "last_norm",
        in_specs=[smem()] + [vmem] * 6 + [pl.BlockSpec(memory_space=pl.ANY)] * len(first_out),
    )(head, gradient, own, recv, tokens, pars[0, 0], routes, *first_out)
    term_list[0] = terms[:4]
    if aligned:
        up_list = add_split(dp_index, up_list, 1, (grad_input,))
        down_list = add_split(dp_index, down_list, 0, (up_list[0][0],))

    terms = jnp.concatenate(term_list, axis=0)
    if not aligned:
        terms = terms.reshape(8 * layers, dp_count, rows)
        terms = lax.all_to_all(jnp.transpose(terms, (1, 0, 2)), "dp", 0, 0, tiled=True)
        terms = lax.psum(jnp.sum(terms, axis=0), "head").reshape(layers, 2, 2, 2, rows)
        grad_gain, grad_bias = terms[:, :, 0], terms[:, :, 1]

    if aligned:
        dims = (
            (layers, rows, 3 * width), (layers, rows, width),
            (layers, 2, rows, hidden_all), (layers, 2, down_rows, width),
        )

        def slot(dims, layer):
            return pl.BlockSpec((1,) + dims[1:], lambda i: (layer,) + (0,) * (len(dims) - 1))

        def unpack(kernel, pieces, old, outs, specs, name, scratch=()):
            return call(
                kernel, [shape(*out, dtype=F32) for out in outs], name,
                grid=(1,),
                in_specs=[smem()] + [whole(*piece.shape) for piece in pieces]
                + [pl.BlockSpec(memory_space=pl.ANY)] * len(old),
                out_specs=specs,
                scratch_shapes=[pltpu.VMEM((4,) + array, BF) for array in scratch],
                input_output_aliases={1 + len(pieces) + at: at for at in range(len(old))},
            )(head, *pieces, *old)

        ffn1 = tie(ffn_shards[1], down_list[0][0])
        up_list = add_split(dp_index, up_list, 2, (ffn1,))
        down_list = add_split(dp_index, down_list, 2, (up_list[0][0],))
        term_lanes = jnp.pad(terms.T.astype(BF), ((0, 0), (0, 128 - terms.shape[0])))
        term_send, term_keep = by_pairs(term_lanes, dp_at, dp_count)
        qkv_send, qkv_keep = attn_grads[0]
        last = [(term_keep, swap(term_send, "dp", 1)), (qkv_keep, swap(qkv_send, "dp", 1))]
        last = add_split(dp_index, last, 1, (down_list[0][0],))
        ffn1 = lax.all_gather(ffn1, "head", axis=0)
        grad_up, grad_down = unpack(
            unpack_later_kernel, [ffn1], (),
            (dims[2], dims[3]), [slot(dims[2], 1), slot(dims[3], 1)], "unpack_later",
        )
        last = add_split(dp_index, last, 2, (grad_up,))
        up0, down0 = add_each([up_list[0], down_list[0]], (last[0][0],))
        down0 = lax.all_gather(down0, "head", axis=0)
        up0 = head_pieces(up0)
        last = head_pieces(add_last(last))
        grad_up, grad_qkv, grad_out = unpack(
            unpack_up_kernel, up0, (grad_up,),
            (dims[2], dims[0], dims[1]), [slot(dims[2], 0), slot(dims[0], 1), slot(dims[1], 1)],
            "unpack_up", [up0[0].shape],
        )
        (grad_down,) = unpack(
            unpack_down_kernel, [down0], (grad_down,), (dims[3],), [slot(dims[3], 0)],
            "unpack_down",
        )
        grad_qkv, grad_out, grad_gain, grad_bias = unpack(
            unpack_attn_kernel, last, (grad_qkv, grad_out),
            (dims[0], dims[1], (layers, 2, 2, rows), (layers, 2, 2, rows)),
            [slot(dims[0], 0), slot(dims[1], 0)] + [whole(layers, 2, 2, rows)] * 2,
            "unpack_attn", [last[0].shape],
        )
        weight_grads = (grad_qkv, grad_out, grad_up, grad_down)
    else:
        grad_qkv, grad_out, grad_up, grad_down = [], [], [], []
        for layer in range(layers):
            attn_shard = lax.psum_scatter(
                attn_grads[layer][0], "dp", scatter_dimension=0, tiled=True
            )
            ffn_all = lax.all_gather(ffn_shards[layer], "head", axis=0)
            attn_all = lax.all_gather(attn_shard, "head", axis=0)
            taken = attn_all[:, :, : 3 * head_cols].reshape(head_count, rows, 3, head_cols)
            grad_qkv.append(jnp.transpose(taken, (1, 2, 0, 3)).reshape(rows, 3 * width))
            taken = jnp.transpose(attn_all[:, :, 3 * head_cols :], (1, 0, 2))
            grad_out.append(taken.reshape(rows, width))
            taken = ffn_all[:, :2].reshape(head_count, 2, rows, dp_count, sub)
            taken = jnp.transpose(taken, (1, 2, 3, 0, 4))
            grad_up.append(taken.reshape(2, rows, hidden_all))
            taken = jnp.transpose(ffn_all[:, 2:], (1, 0, 2, 3))
            grad_down.append(taken.reshape(2, down_rows, width))
        weight_grads = tuple(
            jnp.stack(part).astype(F32) for part in (grad_qkv, grad_out, grad_up, grad_down)
        )
    return (output, grad_input, grad_gain, grad_bias) + weight_grads


def solution(mesh):
    tokens = P(("dp", "head"), None)
    by_dp = (
        P(None, None, None, "dp"),
        P(None, None, None, "dp"),
        P(None, "dp", None),
        P(None, "dp", None),
        P(None, None, "dp", None),
        P(None, None, "dp", None),
    )
    return jax.shard_map(
        body,
        mesh=mesh,
        in_specs=(tokens, P("dp", None), tokens) + by_dp + (tokens,),
        out_specs=(tokens, tokens) + by_dp,
        check_vma=False,
    )
```

```python
import jax
import jax.numpy as jnp
from jax import lax
from jax.experimental import pallas as pl
from jax.experimental.pallas import tpu as pltpu
from jax.sharding import PartitionSpec as P

H = 12
HD = 64
BF = jnp.bfloat16
F32 = jnp.float32
VMEM_BYTES = 50 * 1024 * 1024
COLS = 256
PACKED = 768
KEPT = 640

far_below = -1e30
scale = HD**-0.5


def nn(a, b):
    return lax.dot_general(a, b, (((1,), (0,)), ((), ())), preferred_element_type=F32)


def nt(a, b):
    return lax.dot_general(a, b, (((1,), (1,)), ((), ())), preferred_element_type=F32)


def tn(a, b):
    return lax.dot_general(a, b, (((0,), (0,)), ((), ())), preferred_element_type=F32)


def shape(*dims, dtype=BF):
    return jax.ShapeDtypeStruct(dims, dtype)


def smem():
    return pl.BlockSpec(memory_space=pltpu.SMEM)


def whole(*dims):
    return pl.BlockSpec(dims, lambda i: (0,) * len(dims))


def call(kernel, out_shape, name, micros=0, **rest):
    return pl.pallas_call(
        kernel,
        out_shape=out_shape,
        name=name,
        compiler_params=pltpu.CompilerParams(vmem_limit_bytes=VMEM_BYTES),
        cost_estimate=pl.CostEstimate(
            flops=micros * 1_000_000_000, bytes_accessed=0, transcendentals=0
        ),
        **rest,
    )


def unit_of(values):
    centred = values - jnp.mean(values, axis=-1, keepdims=True)
    inv_std = lax.rsqrt(jnp.mean(centred * centred, axis=-1, keepdims=True) + 1e-05)
    return centred * inv_std, inv_std


def norm_rows(values, par_ref, second):
    gain = jnp.where(second, par_ref[1:2, :], par_ref[0:1, :])
    bias = jnp.where(second, par_ref[3:4, :], par_ref[2:3, :])
    return (unit_of(values)[0] * gain + bias).astype(BF)


def norm_back_rows(grad, incoming, base, par_ref, second, terms_ref):
    unit, inv_std = unit_of(base)
    scaled = incoming * jnp.where(second, par_ref[1:2, :], par_ref[0:1, :])
    fresh = grad + inv_std * (
        scaled
        - jnp.mean(scaled, axis=-1, keepdims=True)
        - unit * jnp.mean(scaled * unit, axis=-1, keepdims=True)
    )
    gain_term = incoming * unit
    zero = jnp.zeros_like(incoming)
    terms_ref[0:1, :] += jnp.sum(jnp.where(second, zero, gain_term), axis=0, keepdims=True)
    terms_ref[1:2, :] += jnp.sum(jnp.where(second, gain_term, zero), axis=0, keepdims=True)
    terms_ref[2:3, :] += jnp.sum(jnp.where(second, zero, incoming), axis=0, keepdims=True)
    terms_ref[3:4, :] += jnp.sum(jnp.where(second, incoming, zero), axis=0, keepdims=True)
    return fresh


def each_block(head, mine_ref, other_ref, act):
    core = head & 1
    pairs, rows = mine_ref.shape[0], mine_ref.shape[1]
    for pair in range(pairs):
        for ref, side in ((mine_ref, core), (other_ref, 1 - core)):
            at = pl.multiple_of((2 * pair + side) * rows, rows)
            act(pl.ds(at, rows), ref[pair].astype(F32))


def split_out(head, total_ref, keep_ref, send_ref):
    core = head & 1
    pairs, rows = keep_ref.shape[0], keep_ref.shape[1]
    for pair in range(pairs):
        at = pl.multiple_of((2 * pair + core) * rows, rows)
        keep_ref[pair] = total_ref[pl.ds(at, rows), :]
        at = pl.multiple_of((2 * pair + 1 - core) * rows, rows)
        send_ref[pair] = total_ref[pl.ds(at, rows), :].astype(BF)


def attend_math(first_ref, w_ref, segc_ref, segr_ref, qkv_ref, attn_ref, lse_ref):
    heads = attn_ref.shape[0] // HD
    qkv = nn(first_ref[...], w_ref[:, : qkv_ref.shape[1]]).astype(BF)
    qkv_ref[...] = qkv
    turned = qkv.T
    same = segc_ref[...] == segr_ref[...]
    for j in range(heads):
        at_q, at_k, at_v = (HD * (j + heads * part) for part in range(3))
        scores = nn(qkv[:, at_k : at_k + HD], turned[at_q : at_q + HD]) * scale
        scores = jnp.where(same, scores, far_below)
        top = jnp.max(scores, axis=0, keepdims=True)
        exponent = jnp.exp(scores - top)
        total = jnp.sum(exponent, axis=0, keepdims=True)
        prob = (exponent / total).astype(BF)
        attn_ref[HD * j : HD * (j + 1), :] = nn(turned[at_v : at_v + HD], prob).astype(BF)
        lse_ref[j : j + 1, :] = top + jnp.log(total)


def join_lanes(blocks_ref, layer, out_ref):
    cols = out_ref.shape[1] // blocks_ref.shape[0]
    for part in range(blocks_ref.shape[0]):
        out_ref[:, part * cols : (part + 1) * cols] = blocks_ref[
            part, :, layer * cols : (layer + 1) * cols
        ]


def attend_first_kernel(
    tok_ref, small_ref, route_ref, w_ref, segc_ref, segr_ref,
    par_ref, first_ref, qkv_ref, attn_ref, lse_ref,
):
    turned = small_ref[...].astype(F32).T
    par_ref[...] = turned[: par_ref.shape[0]]
    first_ref[...] = norm_rows(tok_ref[...].astype(F32), par_ref, route_ref[...] == 1)
    attend_math(first_ref, w_ref, segc_ref, segr_ref, qkv_ref, attn_ref, lse_ref)


def project_kernel(head_ref, attn_ref, wo_ref, keep_ref, send_ref, total_ref, wide_ref):
    join_lanes(wo_ref, 0, wide_ref)
    total_ref[...] = tn(attn_ref[...], wide_ref[...])
    split_out(head_ref[0], total_ref, keep_ref, send_ref)


def attend_kernel(
    layer, head_ref, base_ref, mine_ref, other_ref, par_ref, route_ref, w_ref, wo_ref, segc_ref, segr_ref,
    stream_ref, first_ref, qkv_ref, attn_ref, lse_ref, keep_ref, send_ref, total_ref, wide_ref,
):
    def act(rows, fresh):
        values = base_ref[rows, :].astype(F32) + fresh
        stream_ref[rows, :] = values
        first_ref[rows, :] = norm_rows(values, par_ref, route_ref[rows, :] == 1)

    each_block(head_ref[0], mine_ref, other_ref, act)
    attend_math(first_ref, w_ref, segc_ref, segr_ref, qkv_ref, attn_ref, lse_ref)
    join_lanes(wo_ref, layer, wide_ref)
    total_ref[...] = tn(attn_ref[...], wide_ref[...])
    split_out(head_ref[0], total_ref, keep_ref, send_ref)


def split_sides(dp_ref, bit, grads_ref, send_ref, keep_ref):
    side = (dp_ref[0] >> bit) & 1
    rows = send_ref.shape[-2]
    for out_ref, flip in ((send_ref, 1), (keep_ref, 0)):
        for place in range(out_ref.shape[0]):
            low = place % (1 << bit)
            block = ((place - low) << 1) + low + ((side ^ flip) << bit)
            at = pl.ds(pl.multiple_of(block * rows, 16), rows)
            if len(out_ref.shape) == 3:
                out_ref[place] = grads_ref[at, :]
            else:
                for member in range(out_ref.shape[1]):
                    out_ref[place, member] = grads_ref[member, at, :]


def attend_back_kernel(
    layer, head_ref, grad_ref, mine_ref, other_ref, base_ref, par_ref, route_ref,
    qkv_ref, lse_ref, w_ref, wo_ref, segc_ref, segr_ref,
    fresh_ref, terms_ref, m_ref, gqkv_ref, keep_ref, send_ref, total_ref, turned_ref, wide_ref,
):
    terms_ref[...] = jnp.zeros_like(terms_ref)

    def act(rows, incoming):
        fresh = norm_back_rows(
            grad_ref[rows, :].astype(F32), incoming, base_ref[rows, :].astype(F32),
            par_ref, route_ref[rows, :] == 1, terms_ref,
        )
        fresh_ref[rows, :] = fresh
        m_ref[rows, :] = fresh.astype(BF)

    each_block(head_ref[0], mine_ref, other_ref, act)
    join_lanes(wo_ref, layer, wide_ref)
    heads = wide_ref.shape[0] // HD
    grad_attn = nt(wide_ref[...], m_ref[...]).astype(BF)
    qkv = qkv_ref[...]
    turned = qkv.T
    same = segc_ref[...] == segr_ref[...]
    for j in range(heads):
        at_q, at_k, at_v = (HD * (j + heads * part) for part in range(3))
        scores = nn(qkv[:, at_k : at_k + HD], turned[at_q : at_q + HD]) * scale
        prob = jnp.exp(jnp.where(same, scores, far_below) - lse_ref[j : j + 1, :])
        g_out = grad_attn[HD * j : HD * (j + 1)]
        g_prob = nn(qkv[:, at_v : at_v + HD], g_out)
        inner = jnp.sum(prob * g_prob, axis=0, keepdims=True)
        g_scores = (prob * (g_prob - inner)).astype(BF)
        g_q = nn(turned[at_k : at_k + HD], g_scores) * scale
        g_k = nt(turned[at_q : at_q + HD], g_scores) * scale
        g_v = nt(g_out, prob.astype(BF))
        turned_ref[at_q : at_q + HD, :] = g_q.astype(BF)
        turned_ref[at_k : at_k + HD, :] = g_k.astype(BF)
        turned_ref[at_v : at_v + HD, :] = g_v.astype(BF)
    used = 3 * heads * HD
    turned_ref[used:, :] = jnp.zeros((turned_ref.shape[0] - used, turned_ref.shape[1]), BF)
    g_qkv = turned_ref[...].T
    gqkv_ref[...] = g_qkv
    total_ref[...] = nt(g_qkv, w_ref[:, : g_qkv.shape[1]])
    split_out(head_ref[0], total_ref, keep_ref, send_ref)


def attend_grads_kernel(
    head_ref, dp_ref, first_ref, gqkv_ref, attn_ref, m_ref, after_ref, *rest
):
    zero_ref, *gw_refs, grads_ref = rest
    zero_ref[0, 0] = 0.0
    into_ref = gw_refs[0] if len(gw_refs) == 1 else grads_ref
    cols = into_ref.shape[1] // 4
    grads = tn(first_ref[...], gqkv_ref[...]).astype(BF)
    into_ref[:, : 3 * cols] = grads[:, : 3 * cols]
    for j in range(4):

        @pl.when(head_ref[0] == j)
        def _():
            into_ref[:, 3 * cols :] = nn(
                attn_ref[0], m_ref[:, j * cols : (j + 1) * cols]
            ).astype(BF)

    if len(gw_refs) > 1:
        split_sides(dp_ref, 0, grads_ref, *gw_refs)


def add_up(term, total_ref):
    step = pl.program_id(0)

    @pl.when(step == 0)
    def _():
        total_ref[...] = term

    @pl.when(step > 0)
    def _():
        total_ref[...] += term


def feed_kernel(
    head_ref, base_ref, mine_ref, other_ref, par_ref, route_ref, wu0_ref, wu1_ref, wd0_ref, wd1_ref,
    middle_ref, x_ref, act_ref, slope_ref, keep_ref, send_ref, total_ref,
):
    step = pl.program_id(0)

    @pl.when(step == 0)
    def _():
        def act(rows, fresh):
            values = base_ref[rows, :].astype(F32) + fresh
            middle_ref[rows, :] = values
            x_ref[rows, :] = norm_rows(values, par_ref, route_ref[rows, :] == 1)

        each_block(head_ref[0], mine_ref, other_ref, act)

    second = route_ref[...] == 1
    x = x_ref[...]
    up = jnp.where(second, nn(x, wu1_ref[...]), nn(x, wu0_ref[...]))
    phi = 0.5 * (1.0 + lax.erf(up * 0.7071067811865476))
    active = (up * phi).astype(BF)
    act_ref[...] = active
    slope_ref[...] = (phi + up * jnp.exp(-0.5 * up * up) * 0.3989422804014327).astype(BF)
    zero = jnp.zeros_like(active)
    term = nn(jnp.where(second, zero, active), wd0_ref[...])
    term += nn(jnp.where(second, active, zero), wd1_ref[...])
    add_up(term, total_ref)

    @pl.when(step == pl.num_programs(0) - 1)
    def _():
        split_out(head_ref[0], total_ref, keep_ref, send_ref)


def feed_back_math(
    head_ref, g_ref, slope_ref, wu0_ref, wu1_ref, wd0_ref, wd1_ref, route_ref,
    gup_ref, keep_ref, send_ref, total_ref,
):
    second = route_ref[...] == 1
    g_b = g_ref[...]
    g_up = jnp.where(second, nt(g_b, wd1_ref[...]), nt(g_b, wd0_ref[...]))
    g_up = (g_up * slope_ref[...].astype(F32)).astype(BF)
    gup_ref[...] = g_up
    zero = jnp.zeros_like(g_up)
    term = nt(jnp.where(second, zero, g_up), wu0_ref[...])
    term += nt(jnp.where(second, g_up, zero), wu1_ref[...])
    add_up(term, total_ref)

    @pl.when(pl.program_id(0) == pl.num_programs(0) - 1)
    def _():
        split_out(head_ref[0], total_ref, keep_ref, send_ref)


def feed_back_first_kernel(
    head_ref, g_ref, slope_ref, wu0_ref, wu1_ref, wd0_ref, wd1_ref, route_ref,
    gup_ref, keep_ref, send_ref, total_ref,
):
    feed_back_math(
        head_ref, g_ref, slope_ref, wu0_ref, wu1_ref, wd0_ref, wd1_ref, route_ref,
        gup_ref, keep_ref, send_ref, total_ref,
    )


def feed_back_kernel(
    head_ref, grad_ref, mine_ref, other_ref, base_ref, par_ref,
    slope_ref, wu0_ref, wu1_ref, wd0_ref, wd1_ref, route_ref,
    fresh_ref, terms_ref, g_ref, gup_ref, keep_ref, send_ref, total_ref,
):
    @pl.when(pl.program_id(0) == 0)
    def _():
        terms_ref[...] = jnp.zeros_like(terms_ref)

        def act(rows, incoming):
            fresh = norm_back_rows(
                grad_ref[rows, :], incoming, base_ref[rows, :],
                par_ref, route_ref[rows, :] == 1, terms_ref,
            )
            fresh_ref[rows, :] = fresh
            g_ref[rows, :] = fresh.astype(BF)

        each_block(head_ref[0], mine_ref, other_ref, act)

    feed_back_math(
        head_ref, g_ref, slope_ref, wu0_ref, wu1_ref, wd0_ref, wd1_ref, route_ref,
        gup_ref, keep_ref, send_ref, total_ref,
    )


def feed_grads_kernel(
    carried, dp_ref, g_ref, x_ref, act_ref, gup_ref, route_ref, after_ref, attn_ref, *rest
):
    above, (zero_ref, *outs, turned_ref, grads_ref) = rest[:carried], rest[carried:]
    zero_ref[0, 0] = 0.0
    step = pl.program_id(0)
    cols = act_ref.shape[1]
    second = route_ref[...] == 1

    @pl.when(step == 0)
    def _():
        turned_ref[...] = x_ref[...].T

    into_ref = outs[0] if len(outs) == 1 else grads_ref
    active = act_ref[...]
    g_up = gup_ref[...]
    zero = jnp.zeros_like(g_up)
    here = pl.ds(pl.multiple_of(step * cols, cols), cols)
    for expert in range(2):
        mine = second if expert else jnp.logical_not(second)
        into_ref[expert, :, here] = nn(turned_ref[...], jnp.where(mine, g_up, zero)).astype(BF)
        into_ref[2 + expert, here, :] = tn(jnp.where(mine, active, zero), g_ref[...]).astype(BF)

    @pl.when(step == pl.num_programs(0) - 1)
    def _():
        if len(outs) > 1:
            split_sides(dp_ref, 0, grads_ref.at[:2], outs[0].at[:, :2], outs[1].at[:, :2])
            for from_ref, to_ref in zip(above, outs):
                to_ref[:, 2] = from_ref[...]
            split_sides(dp_ref, 1, grads_ref.at[2:], outs[2], outs[3])


def last_add_kernel(head_ref, middle_ref, own_ref, recv_ref, out_ref):
    rows = out_ref.shape[0]
    at = pl.multiple_of(head_ref[0] * rows, rows)
    out_ref[...] = middle_ref[pl.ds(at, rows), :] + own_ref[...] + recv_ref[...].astype(F32)


def last_norm_kernel(head_ref, grad_ref, own_ref, recv_ref, tok_ref, par_ref, route_ref, *refs):
    out_ref, terms_ref = refs[-2:]
    terms_ref[...] = jnp.zeros_like(terms_ref)
    rows = out_ref.shape[0]
    at = pl.multiple_of(head_ref[0] * rows, rows)
    out_ref[...] = norm_back_rows(
        grad_ref[pl.ds(at, rows), :], own_ref[...] + recv_ref[...].astype(F32),
        tok_ref[...].astype(F32), par_ref, route_ref[...] == 1, terms_ref,
    )


def add_split_kernel(count, bit, dp_ref, *refs):
    inputs, (send_ref, keep_ref) = refs[:count], refs[-2:]
    side = (dp_ref[0] >> bit) & 1
    for out_ref, flip in ((send_ref, 1), (keep_ref, 0)):
        for place in range(out_ref.shape[0]):
            at = 2 * place + (side ^ flip)
            lane = 0
            for one_ref, two_ref in zip(inputs[::2], inputs[1::2]):
                cols = one_ref.shape[-1]
                total = (one_ref[at].astype(F32) + two_ref[at].astype(F32)).astype(BF)
                out_ref[place, ..., lane : lane + cols] = total
                lane += cols


def add_last_kernel(count, *refs):
    inputs, out_ref = refs[:count], refs[-1]
    lane = 0
    for one_ref, two_ref in zip(inputs[::2], inputs[1::2]):
        cols = one_ref.shape[-1]
        total = (one_ref[0].astype(F32) + two_ref[0].astype(F32)).astype(BF)
        out_ref[..., lane : lane + cols] = total
        lane += cols


def add_each_kernel(count, *refs):
    for group in range(count):
        one_ref, two_ref = refs[2 * group : 2 * group + 2]
        total = one_ref[0].astype(F32) + two_ref[0].astype(F32)
        refs[group - count][...] = total.astype(BF)


def tie_kernel(array_ref, after_ref, out_ref):
    pass


def pack_kernel(head_ref, up_ref, down_ref, *refs):
    out_ref, tall_ref = refs[-2:]
    width = down_ref.shape[3]
    count = 4
    hidden = up_ref.shape[3] // count
    sub = down_ref.shape[2] // count
    for j in range(count):

        @pl.when(head_ref[0] == j)
        def _():
            for expert in range(2):
                to = (2 + expert) * hidden
                out_ref[:, to : to + width] = down_ref[0, expert, j * sub : (j + 1) * sub, :]
                for block in range(hidden // sub):
                    at = block * sub * count + j * sub
                    to = expert * hidden + block * sub
                    out_ref[:, to : to + sub] = up_ref[0, expert, :, at : at + sub]
            if out_ref.shape[1] > 4 * hidden:
                qkv_ref, wo_ref, small_ref = refs[:3]
                cols = width // count
                for layer in range(qkv_ref.shape[0]):
                    to = 4 * hidden + layer * PACKED
                    for part in range(3):
                        at = part * width + j * cols
                        out_ref[:, to : to + cols] = qkv_ref[layer, :, at : at + cols]
                        to += cols
                    out_ref[:, to : to + cols] = wo_ref[layer, :, j * cols : (j + 1) * cols]
                tall_ref[...] = jnp.zeros_like(tall_ref)
                tall_ref[: small_ref.shape[0], : small_ref.shape[1]] = small_ref[...].astype(F32)
                out_ref[:, 4 * hidden + qkv_ref.shape[0] * PACKED :] = tall_ref[...].T[
                    : out_ref.shape[0]
                ].astype(BF)


def gather_refs(head_ref, arrays, blocks_ref):
    for s in range(4):
        blocks_ref[head_ref[0] ^ s] = arrays[s][...]


def unpack_up(blocks_ref, gu_ref):
    sub = blocks_ref.shape[2]
    for h in range(4):
        for expert in range(2):
            for block in range(gu_ref.shape[3] // (4 * sub)):
                at = block * 4 * sub + h * sub
                gu_ref[0, expert, :, at : at + sub] = blocks_ref[
                    h, expert, :, block * sub : (block + 1) * sub
                ].astype(F32)


def unpack_down(blocks_ref, first, gd_ref):
    sub = blocks_ref.shape[2]
    for h in range(4):
        for expert in range(2):
            gd_ref[0, expert, h * sub : (h + 1) * sub, :] = blocks_ref[h, first + expert].astype(F32)


def unpack_qkv(block_of, gq_ref, go_ref):
    cols = go_ref.shape[2] // 4
    for h in range(4):
        for part in range(3):
            to = part * 4 * cols + h * cols
            gq_ref[0, :, to : to + cols] = block_of(h, part * cols, cols).astype(F32)
        go_ref[0, :, h * cols : (h + 1) * cols] = block_of(h, 3 * cols, cols).astype(F32)


def unpack_later_kernel(head_ref, ffn_ref, gu_ref, gd_ref):
    unpack_up(ffn_ref, gu_ref)
    unpack_down(ffn_ref, 2, gd_ref)


def unpack_up_kernel(head_ref, *refs):
    gu_ref, gq_ref, go_ref, blocks_ref = refs[-4:]
    gather_refs(head_ref, refs[:4], blocks_ref)
    unpack_up(blocks_ref, gu_ref)
    unpack_qkv(lambda h, at, cols: blocks_ref[h, 2, :, at : at + cols], gq_ref, go_ref)


def unpack_down_kernel(head_ref, blocks_ref, *refs):
    unpack_down(blocks_ref, 0, refs[-1])


def unpack_attn_kernel(head_ref, *refs):
    gq_ref, go_ref, gain_ref, bias_ref, blocks_ref = refs[-5:]
    gather_refs(head_ref, refs[:4], blocks_ref)
    unpack_qkv(lambda h, at, cols: blocks_ref[h, :, 128 + at : 128 + at + cols], gq_ref, go_ref)
    terms = blocks_ref[0, :, :128].astype(F32)
    for h in range(1, 4):
        terms += blocks_ref[h, :, :128].astype(F32)
    turned = terms.T
    for layer in range(2):
        for place in range(2):
            at = 8 * layer + 4 * place
            gain_ref[layer, place] = turned[at : at + 2]
            bias_ref[layer, place] = turned[at + 2 : at + 4]


def swap(array, axis, bits):
    count = lax.axis_size(axis)
    return lax.ppermute(array, axis, [(i, i ^ bits) for i in range(count)])


def half_sum(keep, send):
    return (keep + swap(send, "head", 1).astype(F32)).astype(BF)


def other_half(half, zero=None):
    recv = swap(half, "head", 2).astype(F32)
    if zero is not None:
        recv = recv + zero.reshape(())
    mine = (half.astype(F32) + recv).astype(BF)
    return mine, swap(mine, "head", 1)


def head_sum(keep, send):
    return other_half(half_sum(keep, send))


def own_sum(half, head_at):
    pair = head_at // 2
    recv = swap(lax.dynamic_index_in_dim(half, 1 - pair, 0, keepdims=False).astype(BF), "head", 2)
    return lax.dynamic_index_in_dim(half, pair, 0, keepdims=False), recv


def spread(array, axis):
    copies = jnp.broadcast_to(array[None], (lax.axis_size(axis),) + array.shape)
    return lax.all_to_all(copies, axis, 0, 0, tiled=True)


def head_pieces(shard, after=None):
    across = swap(shard, "head", 2)
    if after is not None:
        across = tie(across, after)
    return [shard, swap(shard, "head", 1), across, swap(across, "head", 1)]


def by_pairs(grads, dp_at, dp_count):
    sides = grads.reshape(dp_count // 2, 2, -1, grads.shape[-1])
    side = dp_at % 2
    return (
        lax.dynamic_index_in_dim(sides, 1 - side, 1, keepdims=False),
        lax.dynamic_index_in_dim(sides, side, 1, keepdims=False),
    )


def add_split(dp_index, lists, bit, after):
    flat = [array for pair in lists for array in pair]
    lanes = sum(keep.shape[-1] for keep, _ in lists)
    dims = (flat[0].shape[0] // 2,) + flat[0].shape[1:-1] + (lanes,)
    vmem = pl.BlockSpec(memory_space=pltpu.VMEM)
    send, keep = call(
        lambda *refs: add_split_kernel(len(flat), bit, *refs), (shape(*dims),) * 2, "add_split",
        in_specs=[smem()] + [vmem] * len(flat) + [pl.BlockSpec(memory_space=pl.ANY)] * len(after),
    )(dp_index, *flat, *after)
    return [(keep, swap(send, "dp", 1 << bit))]


def add_last(lists, after=()):
    flat = [array for pair in lists for array in pair]
    lanes = sum(keep.shape[-1] for keep, _ in lists)
    vmem = pl.BlockSpec(memory_space=pltpu.VMEM)
    return call(
        lambda *refs: add_last_kernel(len(flat), *refs),
        shape(*flat[0].shape[1:-1], lanes), "add_last",
        in_specs=[vmem] * len(flat) + [pl.BlockSpec(memory_space=pl.ANY)] * len(after),
    )(*flat, *after)


def add_each(groups, after):
    flat = [array for pair in groups for array in pair]
    vmem = pl.BlockSpec(memory_space=pltpu.VMEM)
    return call(
        lambda *refs: add_each_kernel(len(groups), *refs),
        [shape(*keep.shape[1:]) for keep, _ in groups], "add_each",
        in_specs=[vmem] * len(flat) + [pl.BlockSpec(memory_space=pl.ANY)] * len(after),
    )(*flat, *after)


def tie(array, after):
    return call(
        tie_kernel, shape(*array.shape), "tie",
        in_specs=[pl.BlockSpec(memory_space=pl.ANY)] * 2,
        out_specs=pl.BlockSpec(memory_space=pl.ANY),
        input_output_aliases={0: 0},
    )(array, after)


def body(tokens, segments, routes, norm_gain, norm_bias, w_qkv, w_out, w_up, w_down, cotangent):
    dp_count = lax.axis_size("dp")
    head_count = lax.axis_size("head")
    head_at = lax.axis_index("head")
    dp_at = lax.axis_index("dp")
    head = head_at.reshape(1)
    dp_index = dp_at.reshape(1)
    tok_count, width = tokens.shape
    row_len = segments.shape[1]
    layers = norm_gain.shape[0]
    head_cols = H // head_count * HD
    hidden_all = w_up.shape[3]
    hidden = hidden_all // head_count
    rows = w_qkv.shape[1]
    down_rows = w_down.shape[2]
    sub = down_rows // head_count
    steps = hidden // COLS
    aligned = rows % 16 == 0 and dp_count == 8 and head_count == 4 and layers == 2

    small = jnp.stack([norm_gain, norm_bias], axis=2).reshape(layers * 8, rows)

    seg_col = segments.reshape(row_len, 1)
    seg_row = segments.reshape(1, row_len)
    route_lanes = jnp.pad(routes.astype(BF), ((0, 0), (0, 127)))
    both = spread(jnp.concatenate([tokens, cotangent, route_lanes], axis=1), "head")
    both = both.reshape(row_len, 2 * width + 128)
    row_tokens = both[:, :width]
    row_cotangent = both[:, width : 2 * width]
    row_routes = both[:, 2 * width : 2 * width + 1].astype(jnp.int32)

    packs = []
    for layer in range(layers):
        extra = (w_qkv, w_out, small) if layer == 0 else ()
        first = (row_tokens, row_cotangent, row_routes) if layer else ()
        lanes = 4 * width + (0 if layer else layers * PACKED + 128)
        if aligned:
            packs.append(
                call(
                    pack_kernel,
                    shape(rows, lanes),
                    "pack",
                    grid=(1,),
                    in_specs=[
                        smem(),
                        pl.BlockSpec(
                            (1, 2, rows, hidden_all), lambda i, layer=layer: (layer, 0, 0, 0)
                        ),
                        pl.BlockSpec(
                            (1, 2, down_rows, width), lambda i, layer=layer: (layer, 0, 0, 0)
                        ),
                    ]
                    + [whole(*array.shape) for array in extra]
                    + [pl.BlockSpec(memory_space=pl.ANY)] * len(first),
                    out_specs=whole(rows, lanes),
                    scratch_shapes=[pltpu.VMEM((128, 128), F32)],
                )(head, w_up, w_down, *extra, *first)
            )
        else:
            taken = lax.dynamic_index_in_dim(
                w_up[layer].reshape(2, rows, dp_count, head_count, sub), head_at, 3, keepdims=False
            ).reshape(2, rows, hidden)
            down = lax.dynamic_index_in_dim(
                w_down[layer].reshape(2, head_count, sub, width), head_at, 1, keepdims=False
            )
            parts = [taken[0], taken[1], down[0], down[1]]
            for at in range(layers if layer == 0 else 0):
                taken = lax.dynamic_index_in_dim(
                    w_qkv[at].reshape(rows, 3, head_count, head_cols), head_at, 2, keepdims=False
                )
                out = lax.dynamic_index_in_dim(
                    w_out[at].reshape(rows, head_count, head_cols), head_at, 1, keepdims=False
                )
                parts += [taken.reshape(rows, 3 * head_cols), out]
            if layer == 0:
                parts.append(jnp.pad(small.T, ((0, 0), (0, 128 - layers * 8))))
            packs.append(jnp.concatenate(parts, axis=1))
    gathered = [lax.all_gather(pack, "dp", axis=0, tiled=True) for pack in packs]
    taken = [
        gathered[0][:, at : at + head_cols]
        for at in (4 * width + layer * PACKED + 3 * head_cols for layer in range(layers))
    ]
    out_w = lax.all_to_all(
        jnp.concatenate(taken, axis=1).reshape(head_count, head_cols, layers * head_cols),
        "head", 0, 0, tiled=True,
    )

    pairs = head_count // 2
    flat = (row_len, width)
    halves = (pairs, tok_count, width)
    both_halves = (shape(*halves, dtype=F32), shape(*halves))
    half_specs = [whole(*halves), whole(*halves)]
    per_expert = width // COLS
    weight_specs = [
        pl.BlockSpec((width, COLS), lambda i: (0, i)),
        pl.BlockSpec((width, COLS), lambda i: (0, per_expert + i)),
        pl.BlockSpec((COLS, width), lambda i: (i, 2)),
        pl.BlockSpec((COLS, width), lambda i: (i, 3)),
    ]
    act_spec = pl.BlockSpec((row_len, COLS), lambda i: (0, i))
    total = pltpu.VMEM(flat, F32)
    vmem = pl.BlockSpec(memory_space=pltpu.VMEM)

    def attn_spec(layer):
        return pl.BlockSpec((width, PACKED), lambda i: (0, 4 * width // PACKED + layer))

    small_spec = pl.BlockSpec((width, 128), lambda i: (0, 4 * width // 128 + layers * PACKED // 128))
    out_spec = whole(head_count, head_cols, layers * head_cols)
    seg_specs = [whole(row_len, 1), whole(1, row_len)]
    wide = pltpu.VMEM((head_cols, width), BF)

    saved = []
    for layer in range(layers):
        kept = (
            shape(*flat), shape(row_len, KEPT), shape(head_cols, row_len),
            shape(8, row_len, dtype=F32),
        )
        kept_specs = [whole(*array.shape) for array in kept]
        if layer == 0:
            stream = row_tokens
            pars, first, qkv, attn, lse = call(
                attend_first_kernel, (shape(layers * 8, width, dtype=F32),) + kept, "attend_first",
                grid=(1,),
                in_specs=[whole(*flat), small_spec, whole(row_len, 1), attn_spec(0)] + seg_specs,
                out_specs=[whole(layers * 8, width)] + kept_specs,
            )(stream, gathered[0], row_routes, gathered[0], seg_col, seg_row)
            pars = pars.reshape(layers, 2, 4, width)
            keep, send = call(
                project_kernel, both_halves, "project",
                in_specs=[smem()] + [vmem] * 2,
                scratch_shapes=[total, wide],
            )(head, attn, out_w)
        else:
            stream, first, qkv, attn, lse, keep, send = call(
                lambda *refs, layer=layer: attend_kernel(layer, *refs),
                (shape(*flat, dtype=F32),) + kept + both_halves,
                "attend",
                grid=(1,),
                in_specs=[smem(), whole(*flat)] + half_specs
                + [whole(4, width), whole(row_len, 1), attn_spec(layer), out_spec] + seg_specs,
                out_specs=[whole(*flat)] + kept_specs + half_specs,
                scratch_shapes=[total, wide],
            )(
                head, middle, mine, other, pars[layer, 0], row_routes, gathered[0], out_w,
                seg_col, seg_row,
            )
        mine, other = head_sum(keep, send)
        middle, second, active, slope, keep, send = call(
            feed_kernel,
            (shape(*flat, dtype=F32), shape(*flat), shape(row_len, hidden), shape(row_len, hidden))
            + both_halves,
            "feed",
            grid=(steps,),
            in_specs=[smem(), whole(*flat)] + half_specs
            + [whole(4, width), whole(row_len, 1)] + weight_specs,
            out_specs=[whole(*flat), whole(*flat), act_spec, act_spec] + half_specs,
            scratch_shapes=[total],
        )(head, stream, mine, other, pars[layer, 1], row_routes, *[gathered[layer]] * 4)
        saved.append((stream, first, qkv, attn, lse, middle, second, active, slope))
        if layer + 1 < layers:
            mine, other = head_sum(keep, send)
    half = keep + swap(send, "head", 1).astype(F32)
    attn_all = lax.all_gather(
        jnp.stack([entry[3] for entry in saved]), "head", axis=1, tiled=True
    )
    own, recv = own_sum(half, head_at)
    output = call(
        last_add_kernel, shape(tok_count, width, dtype=F32), "last_add",
        in_specs=[smem()] + [vmem] * 3,
    )(head, middle, own, recv)

    term_list = [None] * (2 * layers)
    ffn_shards = [None] * layers
    attn_grads = [None] * layers
    markers = {}
    fresh_terms = (shape(*flat, dtype=F32), shape(8, width, dtype=F32))
    whole_grads = (4, width, hidden)
    chunk = (dp_count // 2, 2, rows, width)
    narrow = (dp_count // 2, rows, width)
    gradient = row_cotangent
    for layer in reversed(range(layers)):
        stream, first, qkv, attn, lse, middle, second, active, slope = saved[layer]
        operands = (slope,) + (gathered[layer],) * 4 + (row_routes,)
        operand_specs = [act_spec] + weight_specs + [whole(row_len, 1)]
        if layer == layers - 1:
            grad_b = gradient
            g_up, keep, send = call(
                feed_back_first_kernel, (shape(row_len, hidden),) + both_halves,
                "feed_back_first",
                grid=(steps,),
                in_specs=[smem(), whole(*flat)] + operand_specs,
                out_specs=[act_spec] + half_specs,
                scratch_shapes=[total],
            )(head, gradient, *operands)
        else:
            gradient, terms, grad_b, g_up, keep, send = call(
                feed_back_kernel,
                fresh_terms + (shape(*flat), shape(row_len, hidden)) + both_halves,
                "feed_back",
                grid=(steps,),
                in_specs=[smem(), whole(*flat)] + half_specs
                + [whole(*flat), whole(4, width)] + operand_specs,
                out_specs=[whole(*flat), whole(8, width), whole(*flat), act_spec] + half_specs,
                scratch_shapes=[total],
            )(
                head, gradient, mine, other, saved[layer + 1][0], pars[layer + 1, 0], *operands,
            )
            term_list[2 * layer + 2] = terms[:4] / head_count
        half = half_sum(keep, send)
        by_chunk = aligned and layer == 0
        more = (dp_count // 2, 3, rows, width)
        outs = [more] * 2 + [chunk] * 2 if by_chunk else [whole_grads]
        above = tuple(attn_grads[layer + 1]) if by_chunk else ()
        zero, *ffn_grads = call(
            lambda *refs, count=len(above): feed_grads_kernel(count, *refs),
            (shape(1, 1, dtype=F32),) + tuple(shape(*dims) for dims in outs), "feed_grads",
            grid=(steps,),
            in_specs=[smem(), whole(*flat), whole(*flat), act_spec, act_spec, whole(row_len, 1)]
            + [pl.BlockSpec(memory_space=pl.ANY)] * 2
            + [whole(*array.shape) for array in above],
            out_specs=[smem()] + [whole(*dims) for dims in outs],
            scratch_shapes=[
                pltpu.VMEM((width, row_len), BF),
                pltpu.VMEM(whole_grads if by_chunk else (8, 128), BF),
            ],
        )(dp_index, grad_b, second, active, g_up, row_routes, half, attn_all, *above)
        mine, other = other_half(half, zero)
        if by_chunk:
            up_send, up_keep, down_send, down_keep = ffn_grads
            up_list = [(up_keep, swap(up_send, "dp", 1))]
            down_list = [(down_keep, swap(down_send, "dp", 2))]
        else:
            ffn_shards[layer] = lax.psum_scatter(
                tie(ffn_grads[0], mine), "dp", scatter_dimension=1, tiled=True
            )
        gradient, terms, m_b, g_qkv, keep, send = call(
            lambda *refs, layer=layer: attend_back_kernel(layer, *refs),
            fresh_terms + (shape(*flat), shape(row_len, KEPT)) + both_halves,
            "attend_back",
            grid=(1,),
            in_specs=[smem(), whole(*flat)] + half_specs
            + [whole(*flat), whole(4, width), whole(row_len, 1)]
            + [whole(row_len, KEPT), whole(8, row_len), attn_spec(layer), out_spec] + seg_specs,
            out_specs=[whole(*flat), whole(8, width), whole(*flat), whole(row_len, KEPT)]
            + half_specs,
            scratch_shapes=[total, pltpu.VMEM((KEPT, row_len), BF), wide],
        )(
            head, gradient, mine, other, middle, pars[layer, 1], row_routes,
            qkv, lse, gathered[0], out_w, seg_col, seg_row,
        )
        term_list[2 * layer + 1] = terms[:4] / head_count
        markers["attend", layer] = keep
        if layer:
            half = half_sum(keep, send)
        else:
            half = keep + swap(send, "head", 1).astype(F32)
        outs = [narrow] * 2 if aligned else [(width, width)]
        zero, *qkv_grads = call(
            attend_grads_kernel,
            (shape(1, 1, dtype=F32),) + tuple(shape(*dims) for dims in outs),
            "attend_grads",
            grid=(1,),
            in_specs=[
                smem(), smem(), whole(*flat), whole(row_len, KEPT),
                pl.BlockSpec((1, width, row_len), lambda i, layer=layer: (layer, 0, 0)),
                whole(*flat), pl.BlockSpec(memory_space=pl.ANY),
            ],
            out_specs=[smem()] + [whole(*dims) for dims in outs],
            scratch_shapes=[pltpu.VMEM((width, width), BF)],
        )(head, dp_index, first, g_qkv, attn_all, m_b, half)
        if layer:
            mine, other = other_half(half, zero)
        attn_grads[layer] = qkv_grads
    first_out = ()
    if aligned:
        first_out = (attn_grads[0][0], output)
    own, recv = own_sum(half, head_at)
    grad_input, terms = call(
        last_norm_kernel,
        (shape(tok_count, width, dtype=F32), shape(8, width, dtype=F32)),
        "last_norm",
        in_specs=[smem()] + [vmem] * 6 + [pl.BlockSpec(memory_space=pl.ANY)] * len(first_out),
    )(head, gradient, own, recv, tokens, pars[0, 0], routes, *first_out)
    term_list[0] = terms[:4]
    if aligned:
        up_list = add_split(dp_index, up_list, 1, (grad_input,))
        down_list = add_split(dp_index, down_list, 0, (up_list[0][0],))

    terms = jnp.concatenate(term_list, axis=0)
    if not aligned:
        terms = terms.reshape(8 * layers, dp_count, rows)
        terms = lax.all_to_all(jnp.transpose(terms, (1, 0, 2)), "dp", 0, 0, tiled=True)
        terms = lax.psum(jnp.sum(terms, axis=0), "head").reshape(layers, 2, 2, 2, rows)
        grad_gain, grad_bias = terms[:, :, 0], terms[:, :, 1]

    if aligned:
        dims = (
            (layers, rows, 3 * width), (layers, rows, width),
            (layers, 2, rows, hidden_all), (layers, 2, down_rows, width),
        )

        def slot(dims, layer):
            return pl.BlockSpec((1,) + dims[1:], lambda i: (layer,) + (0,) * (len(dims) - 1))

        def unpack(kernel, pieces, old, outs, specs, name, scratch=()):
            return call(
                kernel, [shape(*out, dtype=F32) for out in outs], name,
                grid=(1,),
                in_specs=[smem()] + [whole(*piece.shape) for piece in pieces]
                + [pl.BlockSpec(memory_space=pl.ANY)] * len(old),
                out_specs=specs,
                scratch_shapes=[pltpu.VMEM((4,) + array, BF) for array in scratch],
                input_output_aliases={1 + len(pieces) + at: at for at in range(len(old))},
            )(head, *pieces, *old)

        ffn1 = tie(ffn_shards[1], down_list[0][0])
        up_list = add_split(dp_index, up_list, 2, (ffn1,))
        down_list = add_split(dp_index, down_list, 2, (up_list[0][0],))
        term_lanes = jnp.pad(terms.T.astype(BF), ((0, 0), (0, 128 - terms.shape[0])))
        term_send, term_keep = by_pairs(term_lanes, dp_at, dp_count)
        qkv_send, qkv_keep = attn_grads[0]
        last = [(term_keep, swap(term_send, "dp", 1)), (qkv_keep, swap(qkv_send, "dp", 1))]
        last = add_split(dp_index, last, 1, (down_list[0][0],))
        ffn1 = lax.all_gather(ffn1, "head", axis=0)
        grad_up, grad_down = unpack(
            unpack_later_kernel, [ffn1], (),
            (dims[2], dims[3]), [slot(dims[2], 1), slot(dims[3], 1)], "unpack_later",
        )
        last = add_split(dp_index, last, 2, (grad_up,))
        up0, down0 = add_each([up_list[0], down_list[0]], (last[0][0],))
        down0 = lax.all_gather(down0, "head", axis=0)
        last = head_pieces(add_last(last))
        up0 = head_pieces(up0, last[2])
        grad_up, grad_qkv, grad_out = unpack(
            unpack_up_kernel, up0, (grad_up,),
            (dims[2], dims[0], dims[1]), [slot(dims[2], 0), slot(dims[0], 1), slot(dims[1], 1)],
            "unpack_up", [up0[0].shape],
        )
        (grad_down,) = unpack(
            unpack_down_kernel, [down0], (grad_down,), (dims[3],), [slot(dims[3], 0)],
            "unpack_down",
        )
        grad_qkv, grad_out, grad_gain, grad_bias = unpack(
            unpack_attn_kernel, last, (grad_qkv, grad_out),
            (dims[0], dims[1], (layers, 2, 2, rows), (layers, 2, 2, rows)),
            [slot(dims[0], 0), slot(dims[1], 0)] + [whole(layers, 2, 2, rows)] * 2,
            "unpack_attn", [last[0].shape],
        )
        weight_grads = (grad_qkv, grad_out, grad_up, grad_down)
    else:
        grad_qkv, grad_out, grad_up, grad_down = [], [], [], []
        for layer in range(layers):
            attn_shard = lax.psum_scatter(
                attn_grads[layer][0], "dp", scatter_dimension=0, tiled=True
            )
            ffn_all = lax.all_gather(ffn_shards[layer], "head", axis=0)
            attn_all = lax.all_gather(attn_shard, "head", axis=0)
            taken = attn_all[:, :, : 3 * head_cols].reshape(head_count, rows, 3, head_cols)
            grad_qkv.append(jnp.transpose(taken, (1, 2, 0, 3)).reshape(rows, 3 * width))
            taken = jnp.transpose(attn_all[:, :, 3 * head_cols :], (1, 0, 2))
            grad_out.append(taken.reshape(rows, width))
            taken = ffn_all[:, :2].reshape(head_count, 2, rows, dp_count, sub)
            taken = jnp.transpose(taken, (1, 2, 3, 0, 4))
            grad_up.append(taken.reshape(2, rows, hidden_all))
            taken = jnp.transpose(ffn_all[:, 2:], (1, 0, 2, 3))
            grad_down.append(taken.reshape(2, down_rows, width))
        weight_grads = tuple(
            jnp.stack(part).astype(F32) for part in (grad_qkv, grad_out, grad_up, grad_down)
        )
    return (output, grad_input, grad_gain, grad_bias) + weight_grads


def solution(mesh):
    tokens = P(("dp", "head"), None)
    by_dp = (
        P(None, None, None, "dp"),
        P(None, None, None, "dp"),
        P(None, "dp", None),
        P(None, "dp", None),
        P(None, None, "dp", None),
        P(None, None, "dp", None),
    )
    return jax.shard_map(
        body,
        mesh=mesh,
        in_specs=(tokens, P("dp", None), tokens) + by_dp + (tokens,),
        out_specs=(tokens, tokens) + by_dp,
        check_vma=False,
    )
```
